32 devices in a mesh: groups: 2 (over y), tm: 4 (over z), sensor: 2 (over x), state: 2 (over core).
Axes of the slice: x: 2, y: 2, z: 4, core: 2. Of those that a mesh axis runs over, the one named last changes fastest.
Arguments:
- obs_rows: bfloat16 [64, 2048, 256], P('groups', ('tm', 'sensor', 'state')), parts along dimension 0, may hold values from -0.375 to 0.375
- readings: float32 [64, 2048], P('groups', ('tm', 'sensor', 'state')), parts along dimension 0, may hold values from -6 to 6
- available: int32 [64, 2048], P('groups', ('tm', 'sensor', 'state')), parts along dimension 0, may hold values 0 or 1
- sensor_ids: int32 [4096], P(('groups', 'tm', 'sensor', 'state')), parts along dimension 0, may hold values from 0 to 2047, each once
- noise_var: float32 [2048], replicated, may hold values from 0.5 to 4
- col_scale: float32 [256], replicated, may hold values from 0.05 to 1
- transition: float32 [256, 256], replicated, may hold values from -0.0025 to 1
- process_info: float32 [256, 256], replicated, may hold values from -3.125 to 1000, as said below
Outputs:
- filtered_mean: float32 [64, 256], P(('groups', 'tm', 'sensor', 'state')), parts along dimension 0
- filtered_cov: float32 [64, 256, 256], P(('groups', 'tm', 'sensor', 'state')), parts along dimension 0
The draws below stay inside these ranges and needn't reach their ends.
There are 2 independent parts, one for each index of `groups`. The reference program is written for one: setup_inputs(seed, part) draws one part's arguments, and reference() takes and returns one part's arrays. A program takes and returns all parts, laid end to end along the dimension named above; an argument that names none is the same for every part. Nothing has to cross between parts.
Inputs may be any that keep to these rules, and one draw needn't show every extreme that they name: `sensor_ids`: each stored column holds a different sensor. `process_info`: symmetric positive definite.
All inputs are finite; a program needn't handle non-finite values. No bound on the sum of `available` on one device may be relied on, other than what follows from the above.
Results may differ from the reference program's by a relative error of at most 0.0043.
Values may be sent and summed in bfloat16 or wider, within the bound.
A program may use at most 128 MiB of HBM per device.

```python
import math
import jax
import jax.numpy as jnp
from jax import lax

DIM = 256
SENSORS = 2048
STEPS = 32


def draw_transition(key, part):
    key = jax.random.fold_in(key, 11)
    rate_key, couple_key = jax.random.split(key)
    decay_rates = jnp.exp(jax.random.uniform(rate_key, (DIM,), jnp.float32, math.log(0.5 / STEPS), math.log(20.0 / STEPS)))
    decay_rates = jnp.minimum(decay_rates, 0.25)
    coupling = jnp.clip(jax.random.normal(couple_key, (DIM, DIM), jnp.float32), -1.75, 1.75) * (0.02 / math.sqrt(DIM))
    coupling = coupling * (1.0 - jnp.eye(DIM, dtype=jnp.float32))
    return jnp.diag(1.0 - decay_rates) + coupling


def draw_process_info(key, part):
    key = jax.random.fold_in(key, 23)
    diag_key, off_key = jax.random.split(key)
    diagonal = jnp.exp(jax.random.uniform(diag_key, (DIM,), jnp.float32, math.log(0.5), math.log(1000.0)))
    raw_values = jnp.clip(jax.random.normal(off_key, (DIM, DIM), jnp.float32) * 0.5, -1.0, 1.0)
    relative = (raw_values + raw_values.T) * (0.4 / DIM) * (1.0 - jnp.eye(DIM, dtype=jnp.float32))
    root_diag = jnp.sqrt(diagonal)
    return jnp.diag(diagonal) + relative * root_diag[:, None] * root_diag[None, :]


def set_ends(values, stream_key, smallest, top_value):
    longest = values.shape.index(max(values.shape))
    spots = []
    for shift in (0, 1):
        where = [jax.random.randint(jax.random.fold_in(stream_key, axis), (), 0, length) for axis, length in enumerate(values.shape)]
        where[longest] = (where[longest] + shift) % values.shape[longest]
        spots.append(tuple(where))
    return values.at[spots[0]].set(smallest).at[spots[1]].set(top_value)


def shard_levels(key, dims, pieces, low, top_value):
    level = 1.0
    for dim, blocks in pieces:
        draws = jax.random.uniform(jax.random.fold_in(jax.random.fold_in(key, 6), dim), (blocks,), jnp.float32, low / len(pieces), top_value / len(pieces))
        level = level * jnp.repeat(jnp.exp(draws), dims[dim] // blocks).reshape((-1,) + (1,) * (len(dims) - 1 - dim))
    return level


def noise(key, dims, scale, most, pieces=(), held_as=jnp.bfloat16):
    entries = jax.random.normal(key, dims, jnp.float32) * scale
    if len(pieces) > 0:
        entries = shard_levels(key, dims, pieces, -0.22, 0.18) * entries
    return jnp.clip(entries, min=-most, max=most).astype(held_as)


def setup_inputs(seed: int = 0, part: int = 0) -> dict:
    key_of = jax.random.split(jax.random.key(seed), 9)
    own_keys = jax.random.split(jax.random.fold_in(key_of[8], part), 9)
    obs_rows = noise(own_keys[0], (STEPS, SENSORS, DIM), DIM ** -0.5, 0.375, ((1, 16),))
    readings = noise(own_keys[1], (STEPS, SENSORS), 1.0, 6.0, ((1, 16),), jnp.float32)
    available = set_ends((jax.random.randint(own_keys[2], (STEPS, SENSORS), 0, 4) < 3).astype(jnp.int32), jax.random.fold_in(own_keys[2], 1), 0, 1)
    sensor_ids = jax.random.permutation(own_keys[3], SENSORS).astype(jnp.int32)
    noise_var = jnp.clip(jnp.exp(jax.random.uniform(key_of[4], (SENSORS,), jnp.float32, math.log(0.5), math.log(4.0))), 0.5, 4.0)
    col_scale = jnp.clip(jnp.exp(jax.random.uniform(key_of[5], (DIM,), jnp.float32, math.log(0.05), math.log(1.0))), 0.05, 1.0)
    transition = draw_transition(jax.random.fold_in(key_of[8], 71), part)
    process_info = draw_process_info(jax.random.fold_in(key_of[8], 71), part)
    return dict(obs_rows=obs_rows, readings=readings, available=available, sensor_ids=sensor_ids, noise_var=noise_var, col_scale=col_scale, transition=transition, process_info=process_info)


highest = lax.Precision.HIGHEST

def matmul(first_op, second_op):
    return jnp.dot(first_op, second_op, precision=highest)

def invert_shifted(matrix):
    factor = jnp.linalg.cholesky(matmul(matrix.T, matrix))
    return jax.scipy.linalg.cho_solve((factor, True), matrix.T)

def build_element(gram_part, info_part, col_scale, transition, process_info, carried, keep_flag):
    state_dim = gram_part.shape[0]
    information = gram_part * (col_scale[:, None] * col_scale[None, :])
    vector = info_part * col_scale
    factor = jnp.linalg.cholesky(process_info + information)
    spread = jax.scipy.linalg.cho_solve((factor, True), jnp.eye(state_dim, dtype=jnp.float32))
    offset = matmul(spread, vector)
    forward = matmul(spread, carried) * keep_flag
    residual = vector - matmul(information, offset)
    backward = matmul(residual, transition) * keep_flag
    inner_term = information - matmul(matmul(information, spread), information)
    precision_part = matmul(matmul(transition.T, inner_term), transition) * keep_flag
    return (forward, offset, spread, backward, precision_part)

def advance(running, element):
    prior_mean, prior_cov = running
    later_a, later_b, later_c, later_e, later_j = element
    state_dim = prior_cov.shape[0]
    shifted = jnp.eye(state_dim, dtype=jnp.float32) + matmul(prior_cov, later_j)
    mixing = matmul(later_a, invert_shifted(shifted))
    new_mean = matmul(mixing, prior_mean + matmul(prior_cov, later_e)) + later_b
    new_cov = matmul(matmul(mixing, prior_cov), later_a.T) + later_c
    return (new_mean, new_cov)

def reference(obs_rows, readings, available, sensor_ids, noise_var, col_scale, transition, process_info):
    weight = available.astype(jnp.float32) * lax.rsqrt(jnp.take(noise_var, sensor_ids))[None, :]
    carried = matmul(process_info, transition)
    keep_flag = (jnp.arange(STEPS) > 0).astype(jnp.float32)

    def per_step(operands):
        row_block, read_row, weight_row, keep_one = operands
        weighted = (row_block.astype(jnp.float32) * weight_row[:, None]).astype(jnp.bfloat16)
        signal = (read_row * weight_row).astype(jnp.bfloat16)
        gram_part = jnp.dot(weighted.T.astype(jnp.float32), weighted.astype(jnp.float32), preferred_element_type=jnp.float32)
        info_part = jnp.dot(signal.astype(jnp.float32), weighted.astype(jnp.float32), preferred_element_type=jnp.float32)
        return build_element(gram_part, info_part, col_scale, transition, process_info, carried, keep_one)
    elements = lax.map(per_step, (obs_rows, readings, weight, keep_flag))

    def step_fn(running, element):
        running = advance(running, element)
        return (running, running)
    start = (jnp.zeros((DIM,), jnp.float32), jnp.zeros((DIM, DIM), jnp.float32))
    unused, outputs = lax.scan(step_fn, start, elements)
    return (outputs[0], outputs[1])
```

```python
import functools

import jax
import jax.numpy as jnp
from jax import lax
from jax.experimental import pallas as pl
from jax.experimental.pallas import tpu as pltpu
from jax.sharding import PartitionSpec as P

highest = lax.Precision.HIGHEST
everyone = ("tm", "sensor", "state")
pad = 8

QUICK_STEPS = 12
SURE_STEPS = 48


def matmul(first_op, second_op):
    return jnp.dot(first_op, second_op, precision=highest)


def full(a, b, ca=1, cb=0):
    return lax.dot_general(
        a, b, (((ca,), (cb,)), ((), ())), precision=highest, preferred_element_type=jnp.float32
    )


def rough(a, b):
    return jnp.dot(
        a.astype(jnp.bfloat16), b.astype(jnp.bfloat16), preferred_element_type=jnp.float32
    )


def identity(n):
    return lax.broadcasted_iota(jnp.int32, (n, n), 0) == lax.broadcasted_iota(
        jnp.int32, (n, n), 1
    )


def invert(matrix, scaled_ref, x_ref):
    n = matrix.shape[0]
    eye = identity(n)
    unit = jnp.where(eye, 1.0, 0.0)
    kept = jnp.where(eye, matrix, 0.0)
    along = lax.rsqrt(jnp.sum(kept, axis=0, keepdims=True))
    down = lax.rsqrt(jnp.sum(kept, axis=1, keepdims=True))
    scaled = matrix * down * along
    scaled_ref[...] = scaled
    alpha = n / jnp.sum(scaled * scaled)
    x_ref[...] = (2.0 * alpha) * unit - (alpha * alpha) * scaled

    def quick(carry):
        count, unused = carry
        x = x_ref[...]
        rest = unit - rough(scaled_ref[...], x)
        size = jnp.sum(rest * rest)
        x_ref[...] = x + rough(x, rest)
        return (count + 1, size)

    unused, size = lax.while_loop(
        lambda c: (c[0] < QUICK_STEPS) & (c[1] > 0.25), quick, (0, jnp.float32(1e3))
    )

    @pl.when(jnp.logical_not(size <= 0.25))
    def _():
        rows = jnp.sum(jnp.abs(scaled_ref[...]), axis=0, keepdims=True)
        x_ref[...] = unit / jnp.max(rows)

    def sure(carry):
        count, unused = carry
        x = x_ref[...]
        rest = unit - full(scaled_ref[...], x)
        size = jnp.sum(rest * rest)
        x_ref[...] = x + full(x, rest + rough(rest, rest))
        return (count + 1, size)

    lax.while_loop(lambda c: (c[0] < SURE_STEPS) & (c[1] > 3e-4), sure, (0, jnp.float32(1e3)))
    return x_ref[...] * down * along


def combine_kernel(flag_ref, a_ref, b_ref, out_ref, scaled_ref, x_ref):
    n = b_ref.shape[1]

    @pl.when(flag_ref[0] == 0)
    def _():
        out_ref[...] = b_ref[...]

    @pl.when(flag_ref[0] != 0)
    def _():
        inverse = invert(a_ref[2 * n : 3 * n] + b_ref[0:n], scaled_ref, x_ref)
        x_ref[...] = inverse
        left = a_ref[n : 2 * n]
        right = b_ref[n : 2 * n]
        left_x = full(left, x_ref[...])
        x_right = full(x_ref[...], right)
        mid = a_ref[3 * n + 1 : 3 * n + 2] + b_ref[3 * n : 3 * n + 1]
        mid = jnp.broadcast_to(mid, (pad, n))
        out_ref[0:n] = a_ref[0:n] - full(left_x, left, 1, 1)
        out_ref[n : 2 * n] = -full(left_x, right)
        out_ref[2 * n : 3 * n] = b_ref[2 * n : 3 * n] - full(right, x_right, 0, 0)
        row = lax.broadcasted_iota(jnp.int32, (pad, n), 0)
        first = a_ref[3 * n : 3 * n + 1] - full(mid, left_x, 1, 1)
        second = b_ref[3 * n + 1 : 3 * n + 2] - full(mid, x_right)
        out_ref[3 * n : 3 * n + pad] = jnp.where(
            row == 0, first, jnp.where(row == 1, second, 0.0)
        )


def advance_into(flag_ref, a_ref, b_ref, out_ref, scaled_ref, x_ref):
    n = b_ref.shape[1]

    @pl.when(flag_ref[0] == 0)
    def _():
        out_ref[...] = b_ref[2 * n : 3 * n + pad]

    @pl.when(flag_ref[0] != 0)
    def _():
        inverse = invert(a_ref[0:n] + b_ref[0:n], scaled_ref, x_ref)
        right = b_ref[n : 2 * n]
        x_right = full(inverse, right)
        mid = a_ref[n + 1 : n + 2] + b_ref[3 * n : 3 * n + 1]
        mid = jnp.broadcast_to(mid, (pad, n))
        out_ref[0:n] = b_ref[2 * n : 3 * n] - full(right, x_right, 0, 0)
        second = b_ref[3 * n + 1 : 3 * n + 2] - full(mid, x_right)
        row = lax.broadcasted_iota(jnp.int32, (pad, n), 0)
        out_ref[n : n + pad] = jnp.where(row == 1, second, 0.0)


def advance_kernel(flag_ref, a_ref, b_ref, out_ref, scaled_ref, x_ref):
    advance_into(flag_ref, a_ref, b_ref, out_ref, scaled_ref, x_ref)


def moments(s_ref, cov_ref, mean_ref, scaled_ref, x_ref):
    n = s_ref.shape[1]
    cov = invert(s_ref[0:n], scaled_ref, x_ref)
    cov_ref[...] = cov
    mean_ref[...] = full(s_ref[n : n + pad], cov, 1, 1)


def moments_kernel(s_ref, cov_ref, mean_ref, scaled_ref, x_ref):
    moments(s_ref, cov_ref, mean_ref, scaled_ref, x_ref)


def last_kernel(flag_ref, a_ref, b_ref, cov_ref, mean_ref, s_ref, scaled_ref, x_ref):
    advance_into(flag_ref, a_ref, b_ref, s_ref, scaled_ref, x_ref)
    moments(s_ref, cov_ref, mean_ref, scaled_ref, x_ref)


vmem = pl.BlockSpec(memory_space=pltpu.VMEM)
smem = pl.BlockSpec(memory_space=pltpu.SMEM)


def call(kernel, specs, shapes, n, *extra):
    return pl.pallas_call(
        kernel,
        out_shape=shapes,
        in_specs=specs,
        out_specs=jax.tree.map(lambda unused: vmem, shapes),
        scratch_shapes=[*extra, pltpu.VMEM((n, n), jnp.float32), pltpu.VMEM((n, n), jnp.float32)],
        compiler_params=pltpu.CompilerParams(vmem_limit_bytes=40 * 1024 * 1024),
        cost_estimate=pl.CostEstimate(flops=20_000_000_000, bytes_accessed=3_000_000, transcendentals=0),
    )


def f32(*shape):
    return jax.ShapeDtypeStruct(shape, jnp.float32)


def combine(flag, earlier, later):
    n = later.shape[1]
    return call(combine_kernel, [smem, vmem, vmem], f32(3 * n + pad, n), n)(flag, earlier, later)


def advance(flag, earlier, later):
    n = later.shape[1]
    return call(advance_kernel, [smem, vmem, vmem], f32(n + pad, n), n)(flag, earlier, later)


def filtered(state):
    n = state.shape[1]
    return call(moments_kernel, [vmem], (f32(n, n), f32(pad, n)), n)(state)


def filtered_after(flag, earlier, later):
    n = later.shape[1]
    return call(
        last_kernel,
        [smem, vmem, vmem],
        (f32(n, n), f32(pad, n)),
        n,
        pltpu.VMEM((n + pad, n), jnp.float32),
    )(flag, earlier, later)


def gram_terms(weighted, signal):
    gram_part = jnp.einsum("tms,tmu->tsu", weighted, weighted, preferred_element_type=jnp.float32)
    info_part = jnp.einsum("tm,tms->ts", signal, weighted, preferred_element_type=jnp.float32)
    return (gram_part, info_part)


def shift_right(x, peers, shift):
    return lax.ppermute(x, everyone, [(k, k + shift) for k in range(peers - shift)])


def body(obs_rows, readings, available, sensor_ids, noise_var, col_scale, transition, process_info):
    n = obs_rows.shape[2]
    sensor_total = noise_var.shape[0]
    lookup_table = (
        sensor_ids[:, None] == jnp.arange(sensor_total, dtype=jnp.int32)[None, :]
    ).astype(jnp.float32)
    local_var = matmul(lookup_table, noise_var)
    weight = available.astype(jnp.float32) * lax.rsqrt(local_var)[None, :]
    weighted = (obs_rows.astype(jnp.float32) * weight[:, :, None]).astype(jnp.bfloat16)
    signal = (readings * weight).astype(jnp.bfloat16)
    arrived = (
        lax.all_to_all(weighted, "tm", split_axis=0, concat_axis=1, tiled=True),
        lax.all_to_all(signal, "tm", split_axis=0, concat_axis=1, tiled=True),
    )
    gram_part, info_part = gram_terms(arrived[0], arrived[1])
    gram_part, info_part = (
        lax.psum_scatter(gram_part, ("sensor", "state"), scatter_dimension=0, tiled=True),
        lax.psum_scatter(info_part, ("sensor", "state"), scatter_dimension=0, tiled=True),
    )
    block_len = gram_part.shape[0]
    peers, mine = lax.axis_size(everyone), lax.axis_index(everyone)
    carried = matmul(process_info, transition)
    inward = matmul(transition.T, carried)
    outer_scale = col_scale[:, None] * col_scale[None, :]

    def element(k):
        keep = (mine * block_len + k > 0).astype(jnp.float32)
        vectors = jnp.concatenate(
            [
                jnp.zeros((1, n), jnp.float32),
                (info_part[k] * col_scale)[None, :],
                jnp.zeros((pad - 2, n), jnp.float32),
            ]
        )
        return jnp.concatenate(
            [
                inward * keep,
                carried.T * -keep,
                process_info + gram_part[k] * outer_scale,
                vectors,
            ]
        )

    elements = [element(k) for k in range(block_len)]
    always = jnp.ones((1,), jnp.int32)
    summary = elements[0]
    for k in range(1, block_len):
        summary = combine(always, summary, elements[k])

    shift = 1
    while 2 * shift < peers:
        summary = combine((mine >= shift).astype(jnp.int32)[None], shift_right(summary, peers, shift), summary)
        shift *= 2
    before = shift_right(summary[2 * n :], peers, shift)
    state = advance((mine >= shift).astype(jnp.int32)[None], before, summary)

    before = shift_right(state, peers, 1)
    covs, means = [], []
    later = (mine > 0).astype(jnp.int32)[None]
    cov_end, mean_end = filtered(state)
    for k in range(block_len - 1):
        cov, mean = filtered_after(later, before, elements[k])
        if k < block_len - 2:
            before = advance(later, before, elements[k])
            later = always
        covs.append(cov)
        means.append(mean[1])
    covs.append(cov_end)
    means.append(mean_end[1])
    return (jnp.stack(means), jnp.stack(covs))


def solution(mesh):
    in_specs = (
        P("groups", ("tm", "sensor", "state"), None),
        P("groups", ("tm", "sensor", "state")),
        P("groups", ("tm", "sensor", "state")),
        P(("groups", "tm", "sensor", "state")),
        P(),
        P(),
        P(),
        P(),
    )
    out_specs = (
        P(("groups", "tm", "sensor", "state"), None),
        P(("groups", "tm", "sensor", "state"), None, None),
    )
    return jax.shard_map(body, mesh=mesh, in_specs=in_specs, out_specs=out_specs, check_vma=False)
```

```python
import jax
import jax.numpy as jnp
from jax import lax
from jax.experimental import pallas as pl
from jax.experimental.pallas import tpu as pltpu
from jax.sharding import PartitionSpec as P

highest = lax.Precision.HIGHEST
everyone = ("tm", "sensor", "state")
pad = 8

QUICK_STEPS = 12
SURE_STEPS = 48


def matmul(first_op, second_op):
    return jnp.dot(first_op, second_op, precision=highest)


def full(a, b, ca=1, cb=0):
    return lax.dot_general(
        a, b, (((ca,), (cb,)), ((), ())), precision=highest, preferred_element_type=jnp.float32
    )


def rough(a, b):
    return jnp.dot(
        a.astype(jnp.bfloat16), b.astype(jnp.bfloat16), preferred_element_type=jnp.float32
    )


def identity(n):
    return lax.broadcasted_iota(jnp.int32, (n, n), 0) == lax.broadcasted_iota(
        jnp.int32, (n, n), 1
    )


def invert(matrix, scaled_ref, x_ref):
    n = matrix.shape[0]
    eye = identity(n)
    unit = jnp.where(eye, 1.0, 0.0)
    kept = jnp.where(eye, matrix, 0.0)
    along = lax.rsqrt(jnp.sum(kept, axis=0, keepdims=True))
    down = lax.rsqrt(jnp.sum(kept, axis=1, keepdims=True))
    scaled = matrix * down * along
    scaled_ref[...] = scaled
    alpha = n / jnp.sum(scaled * scaled)
    x_ref[...] = (2.0 * alpha) * unit - (alpha * alpha) * scaled

    def quick(carry):
        count, unused = carry
        x = x_ref[...]
        rest = unit - rough(scaled_ref[...], x)
        size = jnp.sum(rest * rest)
        x_ref[...] = x + rough(x, rest)
        return (count + 1, size)

    unused, size = lax.while_loop(
        lambda c: (c[0] < QUICK_STEPS) & (c[1] > 0.25), quick, (0, jnp.float32(1e3))
    )

    @pl.when(jnp.logical_not(size <= 0.25))
    def _():
        rows = jnp.sum(jnp.abs(scaled_ref[...]), axis=0, keepdims=True)
        x_ref[...] = unit / jnp.max(rows)

    def sure(carry):
        count, unused = carry
        x = x_ref[...]
        rest = unit - full(scaled_ref[...], x)
        size = jnp.sum(rest * rest)
        x_ref[...] = x + full(x, rest + rough(rest, rest))
        return (count + 1, size)

    lax.while_loop(lambda c: (c[0] < SURE_STEPS) & (c[1] > 3e-4), sure, (0, jnp.float32(1e3)))
    return x_ref[...] * down * along


def combine_into(a_ref, b_ref, out_ref, scaled_ref, x_ref):
    n = b_ref.shape[1]
    inverse = invert(a_ref[2 * n : 3 * n] + b_ref[0:n], scaled_ref, x_ref)
    x_ref[...] = inverse
    left = a_ref[n : 2 * n]
    right = b_ref[n : 2 * n]
    left_x = full(left, x_ref[...])
    x_right = full(x_ref[...], right)
    mid = a_ref[3 * n + 1 : 3 * n + 2] + b_ref[3 * n : 3 * n + 1]
    mid = jnp.broadcast_to(mid, (pad, n))
    out_ref[0:n] = a_ref[0:n] - full(left_x, left, 1, 1)
    out_ref[n : 2 * n] = -full(left_x, right)
    out_ref[2 * n : 3 * n] = b_ref[2 * n : 3 * n] - full(right, x_right, 0, 0)
    row = lax.broadcasted_iota(jnp.int32, (pad, n), 0)
    first = a_ref[3 * n : 3 * n + 1] - full(mid, left_x, 1, 1)
    second = b_ref[3 * n + 1 : 3 * n + 2] - full(mid, x_right)
    out_ref[3 * n : 3 * n + pad] = jnp.where(row == 0, first, jnp.where(row == 1, second, 0.0))


def combine_kernel(flag_ref, a_ref, b_ref, out_ref, scaled_ref, x_ref):
    @pl.when(flag_ref[0] == 0)
    def _():
        out_ref[...] = b_ref[...]

    @pl.when(flag_ref[0] != 0)
    def _():
        combine_into(a_ref, b_ref, out_ref, scaled_ref, x_ref)


def pack_half(core, src, half_ref):
    n = src.shape[1]

    @pl.when(core == 0)
    def _():
        half_ref[0:n] = src[n : 2 * n]
        half_ref[n : n + pad] = src[3 * n : 3 * n + pad]

    @pl.when(core != 0)
    def _():
        down = lax.broadcasted_iota(jnp.int32, (n, n), 0)
        along = lax.broadcasted_iota(jnp.int32, (n, n), 1)
        out = src[2 * n : 3 * n]
        half_ref[0:n] = jnp.where(down <= along, src[0:n], out)
        diagonal = jnp.sum(jnp.where(down == along, out, 0.0), axis=0, keepdims=True)
        row = lax.broadcasted_iota(jnp.int32, (pad, n), 0)
        half_ref[n : n + pad] = jnp.where(row == 2, diagonal, src[3 * n : 3 * n + pad])


def unpack(cross_ref, both_ref, dst):
    n = dst.shape[1]
    down = lax.broadcasted_iota(jnp.int32, (n, n), 0)
    along = lax.broadcasted_iota(jnp.int32, (n, n), 1)
    both = both_ref[0:n]
    flipped = both.T
    dst[0:n] = jnp.where(down <= along, both, flipped)
    dst[n : 2 * n] = cross_ref[0:n]
    out = jnp.where(down > along, both, flipped)
    dst[2 * n : 3 * n] = jnp.where(down == along, both_ref[n + 2 : n + 3], out)
    row = lax.broadcasted_iota(jnp.int32, (pad, n), 0)
    dst[3 * n : 3 * n + pad] = jnp.where(row < 2, both_ref[n : n + pad], 0.0)


def chip_kernel(core_ref, own_ref, other_ref, total_ref, half_ref, scaled_ref, x_ref):
    core = core_ref[0]

    @pl.when(core == 0)
    def _():
        combine_into(own_ref, other_ref, total_ref, scaled_ref, x_ref)

    @pl.when(core != 0)
    def _():
        combine_into(other_ref, own_ref, total_ref, scaled_ref, x_ref)

    pack_half(core, total_ref, half_ref)


def advance_into(a_ref, b_ref, out_ref, scaled_ref, x_ref):
    n = b_ref.shape[1]
    inverse = invert(a_ref[0:n] + b_ref[0:n], scaled_ref, x_ref)
    right = b_ref[n : 2 * n]
    x_right = full(inverse, right)
    mid = a_ref[n + 1 : n + 2] + b_ref[3 * n : 3 * n + 1]
    mid = jnp.broadcast_to(mid, (pad, n))
    out_ref[0:n] = b_ref[2 * n : 3 * n] - full(right, x_right, 0, 0)
    second = b_ref[3 * n + 1 : 3 * n + 2] - full(mid, x_right)
    row = lax.broadcasted_iota(jnp.int32, (pad, n), 0)
    out_ref[n : n + pad] = jnp.where(row == 1, second, 0.0)


def plane_kernel(
    place_ref, mine_ref, theirs_ref, own_ref, group_ref, chip_ref, state_ref, scaled_ref, x_ref
):
    n = own_ref.shape[1]

    @pl.when(place_ref[0] == 0)
    def _():
        unpack(mine_ref, theirs_ref, chip_ref)

    @pl.when(place_ref[0] != 0)
    def _():
        unpack(theirs_ref, mine_ref, chip_ref)

    @pl.when(place_ref[1] == 0)
    def _():
        combine_into(own_ref, chip_ref, group_ref, scaled_ref, x_ref)

    @pl.when(place_ref[1] != 0)
    def _():
        combine_into(chip_ref, own_ref, group_ref, scaled_ref, x_ref)

    state_ref[...] = group_ref[2 * n : 3 * n + pad]


def advance_kernel(flag_ref, a_ref, b_ref, out_ref, scaled_ref, x_ref):
    @pl.when(flag_ref[0] == 0)
    def _():
        n = b_ref.shape[1]
        out_ref[...] = b_ref[2 * n : 3 * n + pad]

    @pl.when(flag_ref[0] != 0)
    def _():
        advance_into(a_ref, b_ref, out_ref, scaled_ref, x_ref)


def last_kernel(flag_ref, a_ref, b_ref, c_ref, cov_ref, mean_ref, s_ref, scaled_ref, x_ref):
    n = a_ref.shape[1]
    for k, e_ref in enumerate((b_ref, c_ref)):

        @pl.when(flag_ref[0] == 0)
        def _():
            s_ref[...] = e_ref[2 * n : 3 * n + pad]

        @pl.when(flag_ref[0] != 0)
        def _():
            advance_into(a_ref, e_ref, s_ref, scaled_ref, x_ref)

        cov = invert(s_ref[0:n], scaled_ref, x_ref)
        cov_ref[k] = cov
        mean_ref[k] = full(s_ref[n : n + pad], cov, 1, 1)


vmem = pl.BlockSpec(memory_space=pltpu.VMEM)
smem = pl.BlockSpec(memory_space=pltpu.SMEM)


def call(kernel, specs, shapes, n, *extra):
    return pl.pallas_call(
        kernel,
        out_shape=shapes,
        in_specs=specs,
        out_specs=jax.tree.map(lambda unused: vmem, shapes),
        scratch_shapes=[*extra, pltpu.VMEM((n, n), jnp.float32), pltpu.VMEM((n, n), jnp.float32)],
        compiler_params=pltpu.CompilerParams(vmem_limit_bytes=40 * 1024 * 1024),
        cost_estimate=pl.CostEstimate(flops=20_000_000_000, bytes_accessed=3_000_000, transcendentals=0),
    )


def f32(*shape):
    return jax.ShapeDtypeStruct(shape, jnp.float32)


def combine(flag, earlier, later):
    n = later.shape[1]
    return call(combine_kernel, [smem, vmem, vmem], f32(3 * n + pad, n), n)(flag, earlier, later)


def advance(flag, earlier, later):
    n = later.shape[1]
    return call(advance_kernel, [smem, vmem, vmem], f32(n + pad, n), n)(flag, earlier, later)


def chip_total(core, own, other):
    n = own.shape[1]
    shapes = (f32(3 * n + pad, n), f32(n + pad, n))
    return call(chip_kernel, [smem, vmem, vmem], shapes, n)(core, own, other)


def plane_total(place, mine, theirs, own):
    n = own.shape[1]
    shapes = (f32(3 * n + pad, n), f32(3 * n + pad, n), f32(n + pad, n))
    return call(plane_kernel, [smem, vmem, vmem, vmem], shapes, n)(place, mine, theirs, own)


def filtered(flag, earlier, first, second):
    n = earlier.shape[1]
    return call(
        last_kernel,
        [smem, vmem, vmem, vmem],
        (f32(2, n, n), f32(2, pad, n)),
        n,
        pltpu.VMEM((n + pad, n), jnp.float32),
    )(flag, earlier, first, second)


def gram_terms(weighted):
    gram_part = jnp.einsum("tms,tmu->tsu", weighted, weighted, preferred_element_type=jnp.float32)
    return gram_part


def swap(x, axis):
    return lax.ppermute(x, axis, [(0, 1), (1, 0)])


def flag(*values):
    return jnp.stack([jnp.asarray(value, jnp.int32) for value in values])


def body(obs_rows, readings, available, sensor_ids, noise_var, col_scale, transition, process_info):
    n = obs_rows.shape[2]
    sensor_total = noise_var.shape[0]
    lookup_table = (
        sensor_ids[:, None] == jnp.arange(sensor_total, dtype=jnp.int32)[None, :]
    ).astype(jnp.float32)
    local_var = matmul(lookup_table, noise_var)
    weight = available.astype(jnp.float32) * lax.rsqrt(local_var)[None, :]
    weighted = (obs_rows.astype(jnp.float32) * weight[:, :, None]).astype(jnp.bfloat16)
    signal = (readings * weight).astype(jnp.bfloat16)
    own_info = jnp.einsum("tm,tms->ts", signal, weighted, preferred_element_type=jnp.float32)
    info_part = lax.psum_scatter(own_info, everyone, scatter_dimension=0, tiled=True)
    arrived = lax.all_to_all(weighted, "tm", split_axis=0, concat_axis=1, tiled=True)
    gram_part = lax.psum_scatter(
        gram_terms(arrived), ("sensor", "state"), scatter_dimension=0, tiled=True
    )
    block_len = gram_part.shape[0]
    mine = lax.axis_index(everyone)
    carried = matmul(process_info, transition)
    inward = matmul(transition.T, carried)
    outer_scale = col_scale[:, None] * col_scale[None, :]

    def element(k):
        keep = (mine * block_len + k > 0).astype(jnp.float32)
        vectors = jnp.concatenate(
            [
                jnp.zeros((1, n), jnp.float32),
                (info_part[k] * col_scale)[None, :],
                jnp.zeros((pad - 2, n), jnp.float32),
            ]
        )
        return jnp.concatenate(
            [
                inward * keep,
                carried.T * -keep,
                process_info + gram_part[k] * outer_scale,
                vectors,
            ]
        )

    elements = [element(k) for k in range(block_len)]
    summary = combine(flag(1), elements[0], elements[1])

    core = lax.axis_index("state")
    chips, chip = lax.axis_size("sensor"), lax.axis_index("sensor")
    planes, plane = lax.axis_size("tm"), lax.axis_index("tm")
    other = swap(summary, "state")
    own_chip, half = chip_total(flag(core), summary, other)
    if chips == 2:
        mine_half = swap(half, "sensor")
        theirs_half = swap(mine_half, "state")
        group, prior, state = plane_total(flag(core, chip), mine_half, theirs_half, own_chip)
        has_prior = chip > 0
    else:
        everything = lax.all_gather(own_chip, "sensor")
        group, prior = everything[0], everything[0]
        for k in range(1, chips):
            group = combine(flag(1), group, everything[k])
            if k < chips - 1:
                prior = jnp.where(k < chip, group, prior)
        has_prior = chip > 0
        state = group[2 * n :]

    incoming = jnp.zeros_like(state)
    for k in range(1, planes):
        perm = [(k - 1, k)]
        came = lax.ppermute(state, "tm", perm)
        if k < planes - 1:
            state = advance(flag(plane == k), came, group)
        incoming = incoming + came

    ahead = combine(flag(has_prior & (core > 0)), prior, other)
    ahead = jnp.where(core > 0, ahead, prior)
    has_ahead = has_prior | (core > 0)
    first = combine(flag(has_ahead), ahead, elements[0])
    second = combine(flag(has_ahead), ahead, summary)
    covs, means = filtered(flag(plane > 0), incoming, first, second)
    return (means[:, 1], covs)


def solution(mesh):
    in_specs = (
        P("groups", ("tm", "sensor", "state"), None),
        P("groups", ("tm", "sensor", "state")),
        P("groups", ("tm", "sensor", "state")),
        P(("groups", "tm", "sensor", "state")),
        P(),
        P(),
        P(),
        P(),
    )
    out_specs = (
        P(("groups", "tm", "sensor", "state"), None),
        P(("groups", "tm", "sensor", "state"), None, None),
    )
    return jax.shard_map(body, mesh=mesh, in_specs=in_specs, out_specs=out_specs, check_vma=False)
```

```python
import jax
import jax.numpy as jnp
from jax import lax
from jax.experimental import pallas as pl
from jax.experimental.pallas import tpu as pltpu
from jax.sharding import PartitionSpec as P

highest = lax.Precision.HIGHEST
everyone = ("tm", "sensor", "state")
pad = 8
extra = 16

QUICK_STEPS = 12
SURE_STEPS = 48


def matmul(first_op, second_op):
    return jnp.dot(first_op, second_op, precision=highest)


def full(a, b, ca=1, cb=0):
    return lax.dot_general(
        a, b, (((ca,), (cb,)), ((), ())), precision=highest, preferred_element_type=jnp.float32
    )


def rough(a, b):
    return jnp.dot(
        a.astype(jnp.bfloat16), b.astype(jnp.bfloat16), preferred_element_type=jnp.float32
    )


def identity(n):
    return lax.broadcasted_iota(jnp.int32, (n, n), 0) == lax.broadcasted_iota(
        jnp.int32, (n, n), 1
    )


def invert(matrix, scaled_ref, x_ref):
    n = matrix.shape[0]
    eye = identity(n)
    unit = jnp.where(eye, 1.0, 0.0)
    kept = jnp.where(eye, matrix, 0.0)
    along = lax.rsqrt(jnp.sum(kept, axis=0, keepdims=True))
    down = lax.rsqrt(jnp.sum(kept, axis=1, keepdims=True))
    scaled = matrix * down * along
    scaled_ref[...] = scaled
    alpha = n / jnp.sum(scaled * scaled)
    x_ref[...] = (2.0 * alpha) * unit - (alpha * alpha) * scaled

    def quick(carry):
        count, unused = carry
        x = x_ref[...]
        rest = unit - rough(scaled_ref[...], x)
        size = jnp.sum(rest * rest)
        x_ref[...] = x + rough(x, rest)
        return (count + 1, size)

    unused, size = lax.while_loop(
        lambda c: (c[0] < QUICK_STEPS) & (c[1] > 0.25), quick, (0, jnp.float32(1e3))
    )

    @pl.when(jnp.logical_not(size <= 0.25))
    def _():
        rows = jnp.sum(jnp.abs(scaled_ref[...]), axis=0, keepdims=True)
        x_ref[...] = unit / jnp.max(rows)

    def sure(carry):
        count, unused = carry
        x = x_ref[...]
        rest = unit - full(scaled_ref[...], x)
        size = jnp.sum(rest * rest)
        x_ref[...] = x + full(x, rest + rough(rest, rest))
        return (count + 1, size)

    lax.while_loop(lambda c: (c[0] < SURE_STEPS) & (c[1] > 3e-4), sure, (0, jnp.float32(1e3)))
    return x_ref[...] * down * along


def combine_into(a_ref, b_ref, out_ref, scaled_ref, x_ref):
    n = b_ref.shape[1]
    inverse = invert(a_ref[2 * n : 3 * n] + b_ref[0:n], scaled_ref, x_ref)
    x_ref[...] = inverse
    left = a_ref[n : 2 * n]
    right = b_ref[n : 2 * n]
    left_x = full(left, x_ref[...])
    x_right = full(x_ref[...], right)
    mid = a_ref[3 * n + 1 : 3 * n + 2] + b_ref[3 * n : 3 * n + 1]
    mid = jnp.broadcast_to(mid, (pad, n))
    out_ref[0:n] = a_ref[0:n] - full(left_x, left, 1, 1)
    out_ref[n : 2 * n] = -full(left_x, right)
    out_ref[2 * n : 3 * n] = b_ref[2 * n : 3 * n] - full(right, x_right, 0, 0)
    row = lax.broadcasted_iota(jnp.int32, (pad, n), 0)
    first = a_ref[3 * n : 3 * n + 1] - full(mid, left_x, 1, 1)
    second = b_ref[3 * n + 1 : 3 * n + 2] - full(mid, x_right)
    out_ref[3 * n : 3 * n + pad] = jnp.where(row == 0, first, jnp.where(row == 1, second, 0.0))


def combine_kernel(flag_ref, a_ref, b_ref, out_ref, scaled_ref, x_ref):
    @pl.when(flag_ref[0] == 0)
    def _():
        out_ref[...] = b_ref[...]

    @pl.when(flag_ref[0] != 0)
    def _():
        combine_into(a_ref, b_ref, out_ref, scaled_ref, x_ref)


def pack_half(core, src, half_ref):
    n = src.shape[1]

    @pl.when(core == 0)
    def _():
        half_ref[0:n] = src[n : 2 * n]
        half_ref[n : n + pad] = src[3 * n : 3 * n + pad]

    @pl.when(core != 0)
    def _():
        down = lax.broadcasted_iota(jnp.int32, (n, n), 0)
        along = lax.broadcasted_iota(jnp.int32, (n, n), 1)
        out = src[2 * n : 3 * n]
        half_ref[0:n] = jnp.where(down <= along, src[0:n], out)
        diagonal = jnp.sum(jnp.where(down == along, out, 0.0), axis=0, keepdims=True)
        row = lax.broadcasted_iota(jnp.int32, (pad, n), 0)
        half_ref[n : n + pad] = jnp.where(row == 2, diagonal, src[3 * n : 3 * n + pad])


def unpack(cross_ref, both_ref, dst):
    n = dst.shape[1]
    down = lax.broadcasted_iota(jnp.int32, (n, n), 0)
    along = lax.broadcasted_iota(jnp.int32, (n, n), 1)
    both = both_ref[0:n]
    flipped = both.T
    dst[0:n] = jnp.where(down <= along, both, flipped)
    dst[n : 2 * n] = cross_ref[0:n]
    out = jnp.where(down > along, both, flipped)
    dst[2 * n : 3 * n] = jnp.where(down == along, both_ref[n + 2 : n + 3], out)
    row = lax.broadcasted_iota(jnp.int32, (pad, n), 0)
    dst[3 * n : 3 * n + pad] = jnp.where(row < 2, both_ref[n : n + pad], 0.0)


def chip_kernel(core_ref, own_ref, other_ref, total_ref, half_ref, scaled_ref, x_ref):
    core = core_ref[0]

    @pl.when(core == 0)
    def _():
        combine_into(own_ref, other_ref, total_ref, scaled_ref, x_ref)

    @pl.when(core != 0)
    def _():
        combine_into(other_ref, own_ref, total_ref, scaled_ref, x_ref)

    pack_half(core, total_ref, half_ref)


def advance_into(a_ref, b_ref, out_ref, scaled_ref, x_ref):
    n = b_ref.shape[1]
    inverse = invert(a_ref[0:n] + b_ref[0:n], scaled_ref, x_ref)
    right = b_ref[n : 2 * n]
    x_right = full(inverse, right)
    mid = a_ref[n + 1 : n + 2] + b_ref[3 * n : 3 * n + 1]
    mid = jnp.broadcast_to(mid, (pad, n))
    out_ref[0:n] = b_ref[2 * n : 3 * n] - full(right, x_right, 0, 0)
    second = b_ref[3 * n + 1 : 3 * n + 2] - full(mid, x_right)
    row = lax.broadcasted_iota(jnp.int32, (pad, n), 0)
    out_ref[n : n + pad] = jnp.where(row == 1, second, 0.0)


def plane_kernel(
    place_ref, mine_ref, theirs_ref, own_ref, group_ref, chip_ref, state_ref, scaled_ref, x_ref
):
    n = own_ref.shape[1]

    @pl.when(place_ref[0] == 0)
    def _():
        unpack(mine_ref, theirs_ref, chip_ref)

    @pl.when(place_ref[0] != 0)
    def _():
        unpack(theirs_ref, mine_ref, chip_ref)

    @pl.when(place_ref[1] == 0)
    def _():
        combine_into(own_ref, chip_ref, group_ref, scaled_ref, x_ref)

    @pl.when(place_ref[1] != 0)
    def _():
        combine_into(chip_ref, own_ref, group_ref, scaled_ref, x_ref)

    state_ref[...] = group_ref[2 * n : 3 * n + pad]


def advance_kernel(flag_ref, a_ref, b_ref, out_ref, scaled_ref, x_ref):
    @pl.when(flag_ref[0] == 0)
    def _():
        n = b_ref.shape[1]
        out_ref[...] = b_ref[2 * n : 3 * n + pad]

    @pl.when(flag_ref[0] != 0)
    def _():
        advance_into(a_ref, b_ref, out_ref, scaled_ref, x_ref)


def last_kernel(flag_ref, a_ref, b_ref, c_ref, cov_ref, mean_ref, s_ref, scaled_ref, x_ref):
    n = a_ref.shape[1]
    for k, e_ref in enumerate((b_ref, c_ref)):

        @pl.when(flag_ref[0] == 0)
        def _():
            s_ref[...] = e_ref[2 * n : 3 * n + pad]

        @pl.when(flag_ref[0] != 0)
        def _():
            advance_into(a_ref, e_ref, s_ref, scaled_ref, x_ref)

        cov = invert(s_ref[0:n], scaled_ref, x_ref)
        cov_ref[k] = cov
        mean_ref[k] = full(s_ref[n : n + pad], cov, 1, 1)


vmem = pl.BlockSpec(memory_space=pltpu.VMEM)
smem = pl.BlockSpec(memory_space=pltpu.SMEM)


def call(kernel, specs, shapes, n, *extra):
    return pl.pallas_call(
        kernel,
        out_shape=shapes,
        in_specs=specs,
        out_specs=jax.tree.map(lambda unused: vmem, shapes),
        scratch_shapes=[*extra, pltpu.VMEM((n, n), jnp.float32), pltpu.VMEM((n, n), jnp.float32)],
        compiler_params=pltpu.CompilerParams(vmem_limit_bytes=40 * 1024 * 1024),
        cost_estimate=pl.CostEstimate(flops=20_000_000_000, bytes_accessed=3_000_000, transcendentals=0),
    )


def f32(*shape):
    return jax.ShapeDtypeStruct(shape, jnp.float32)


def combine(flag, earlier, later):
    n = later.shape[1]
    return call(combine_kernel, [smem, vmem, vmem], f32(3 * n + pad, n), n)(flag, earlier, later)


def advance(flag, earlier, later):
    n = later.shape[1]
    return call(advance_kernel, [smem, vmem, vmem], f32(n + pad, n), n)(flag, earlier, later)


def chip_total(core, own, other):
    n = own.shape[1]
    shapes = (f32(3 * n + pad, n), f32(n + pad, n))
    return call(chip_kernel, [smem, vmem, vmem], shapes, n)(core, own, other)


def plane_total(place, mine, theirs, own):
    n = own.shape[1]
    shapes = (f32(3 * n + pad, n), f32(3 * n + pad, n), f32(n + pad, n))
    return call(plane_kernel, [smem, vmem, vmem, vmem], shapes, n)(place, mine, theirs, own)


def filtered(flag, earlier, first, second):
    n = earlier.shape[1]
    return call(
        last_kernel,
        [smem, vmem, vmem, vmem],
        (f32(2, n, n), f32(2, pad, n)),
        n,
        pltpu.VMEM((n + pad, n), jnp.float32),
    )(flag, earlier, first, second)


def gram_kernel(x_ref, out_ref):
    peers, n = x_ref.shape[1], x_ref.shape[4]
    sensors = x_ref.shape[3] - extra
    half = n // 2
    rows = x_ref[0, :, 0, 0:sensors, :].reshape(peers * sensors, n)
    gram = lax.dot_general(
        rows, rows, (((0,), (0,)), ((), ())), preferred_element_type=jnp.float32
    )
    out_ref[0, 0, 0:half] = gram[0:half]
    out_ref[0, 0, half : half + half // 2, 0:half] = gram[half : half + half // 2, half:]
    out_ref[0, 0, half : half + half // 2, half:] = gram[half + half // 2 :, half:]
    tail = x_ref[0, :, 0, sensors:, :].astype(jnp.float32).reshape(peers * extra, n)
    info = jnp.sum(tail, axis=0, keepdims=True)
    out_ref[0, 0, half + half // 2 :] = jnp.broadcast_to(info, (pad, n))


def gram_terms(rows):
    blocks, peers, steps, height, n = rows.shape
    tall = n // 2 + n // 4 + pad
    return pl.pallas_call(
        gram_kernel,
        grid=(blocks, steps),
        out_shape=f32(blocks, steps, tall, n),
        in_specs=[pl.BlockSpec((1, peers, 1, height, n), lambda i, j: (i, 0, j, 0, 0))],
        out_specs=pl.BlockSpec((1, 1, tall, n), lambda i, j: (i, j, 0, 0)),
        compiler_params=pltpu.CompilerParams(vmem_limit_bytes=24 * 1024 * 1024),
    )(rows)


def whole_gram(packed):
    n = packed.shape[1]
    half, quarter = n // 2, n // 4
    low = packed[half : half + quarter]
    corner = jnp.concatenate([low[:, :half], low[:, half:]], axis=0)
    top = packed[:half]
    return jnp.concatenate([top, jnp.concatenate([top[:, half:].T, corner], axis=1)], axis=0)


def three_terms(x):
    high = lax.reduce_precision(x, 8, 7)
    rest = x - high
    middle = lax.reduce_precision(rest, 8, 7)
    return jnp.stack([high, middle, rest - middle], axis=1).astype(jnp.bfloat16)


def swap(x, axis):
    return lax.ppermute(x, axis, [(0, 1), (1, 0)])


def flag(*values):
    return jnp.stack([jnp.asarray(value, jnp.int32) for value in values])


def body(obs_rows, readings, available, sensor_ids, noise_var, col_scale, transition, process_info):
    n = obs_rows.shape[2]
    sensor_total = noise_var.shape[0]
    lookup_table = (
        sensor_ids[:, None] == jnp.arange(sensor_total, dtype=jnp.int32)[None, :]
    ).astype(jnp.float32)
    local_var = matmul(lookup_table, noise_var)
    weight = available.astype(jnp.float32) * lax.rsqrt(local_var)[None, :]
    weighted = (obs_rows.astype(jnp.float32) * weight[:, :, None]).astype(jnp.bfloat16)
    signal = (readings * weight).astype(jnp.bfloat16)
    own_info = jnp.einsum("tm,tms->ts", signal, weighted, preferred_element_type=jnp.float32)
    steps = obs_rows.shape[0]
    planes, plane_size = lax.axis_size("tm"), lax.axis_size(("sensor", "state"))
    block_len = steps // (planes * plane_size)
    terms = three_terms(own_info)
    terms = jnp.pad(terms, ((0, 0), (0, extra - terms.shape[1]), (0, 0)))
    sent = jnp.concatenate([weighted, terms], axis=1)
    sent = sent.reshape(planes, plane_size, block_len, sent.shape[1], n)
    arrived = lax.all_to_all(sent, ("sensor", "state"), split_axis=1, concat_axis=1, tiled=True)
    packed = lax.psum_scatter(gram_terms(arrived), "tm", scatter_dimension=0, tiled=True)[0]
    gram_part = [whole_gram(packed[k]) for k in range(block_len)]
    info_part = packed[:, n // 2 + n // 4]
    mine = lax.axis_index(everyone)
    carried = matmul(process_info, transition)
    inward = matmul(transition.T, carried)
    outer_scale = col_scale[:, None] * col_scale[None, :]

    def element(k):
        keep = (mine * block_len + k > 0).astype(jnp.float32)
        vectors = jnp.concatenate(
            [
                jnp.zeros((1, n), jnp.float32),
                (info_part[k] * col_scale)[None, :],
                jnp.zeros((pad - 2, n), jnp.float32),
            ]
        )
        return jnp.concatenate(
            [
                inward * keep,
                carried.T * -keep,
                process_info + gram_part[k] * outer_scale,
                vectors,
            ]
        )

    elements = [element(k) for k in range(block_len)]
    summary = combine(flag(1), elements[0], elements[1])

    core = lax.axis_index("state")
    chips, chip = lax.axis_size("sensor"), lax.axis_index("sensor")
    planes, plane = lax.axis_size("tm"), lax.axis_index("tm")
    other = swap(summary, "state")
    own_chip, half = chip_total(flag(core), summary, other)
    if chips == 2:
        mine_half = swap(half, "sensor")
        theirs_half = swap(mine_half, "state")
        group, prior, state = plane_total(flag(core, chip), mine_half, theirs_half, own_chip)
        has_prior = chip > 0
    else:
        everything = lax.all_gather(own_chip, "sensor")
        group, prior = everything[0], everything[0]
        for k in range(1, chips):
            group = combine(flag(1), group, everything[k])
            if k < chips - 1:
                prior = jnp.where(k < chip, group, prior)
        has_prior = chip > 0
        state = group[2 * n :]

    incoming = jnp.zeros_like(state)
    for k in range(1, planes):
        perm = [(k - 1, k)]
        came = lax.ppermute(state, "tm", perm)
        if k < planes - 1:
            state = advance(flag(plane == k), came, group)
        incoming = incoming + came

    ahead = combine(flag(has_prior & (core > 0)), prior, other)
    ahead = jnp.where(core > 0, ahead, prior)
    has_ahead = has_prior | (core > 0)
    first = combine(flag(has_ahead), ahead, elements[0])
    second = combine(flag(has_ahead), ahead, summary)
    covs, means = filtered(flag(plane > 0), incoming, first, second)
    return (means[:, 1], covs)


def solution(mesh):
    in_specs = (
        P("groups", ("tm", "sensor", "state"), None),
        P("groups", ("tm", "sensor", "state")),
        P("groups", ("tm", "sensor", "state")),
        P(("groups", "tm", "sensor", "state")),
        P(),
        P(),
        P(),
        P(),
    )
    out_specs = (
        P(("groups", "tm", "sensor", "state"), None),
        P(("groups", "tm", "sensor", "state"), None, None),
    )
    return jax.shard_map(body, mesh=mesh, in_specs=in_specs, out_specs=out_specs, check_vma=False)
```

```python
import jax
import jax.numpy as jnp
from jax import lax
from jax.experimental import pallas as pl
from jax.experimental.pallas import tpu as pltpu
from jax.sharding import PartitionSpec as P

highest = lax.Precision.HIGHEST
everyone = ("tm", "sensor", "state")
pad = 8
extra = 16

QUICK_STEPS = 12
SURE_STEPS = 48


def matmul(first_op, second_op):
    return jnp.dot(first_op, second_op, precision=highest)


def full(a, b, ca=1, cb=0):
    return lax.dot_general(
        a, b, (((ca,), (cb,)), ((), ())), precision=highest, preferred_element_type=jnp.float32
    )


def rough(a, b):
    return jnp.dot(
        a.astype(jnp.bfloat16), b.astype(jnp.bfloat16), preferred_element_type=jnp.float32
    )


def identity(n):
    return lax.broadcasted_iota(jnp.int32, (n, n), 0) == lax.broadcasted_iota(
        jnp.int32, (n, n), 1
    )


def invert(matrix, scaled_ref, x_ref):
    n = matrix.shape[0]
    eye = identity(n)
    unit = jnp.where(eye, 1.0, 0.0)
    kept = jnp.where(eye, matrix, 0.0)
    along = lax.rsqrt(jnp.sum(kept, axis=0, keepdims=True))
    down = lax.rsqrt(jnp.sum(kept, axis=1, keepdims=True))
    scaled = matrix * down * along
    scaled_ref[...] = scaled
    alpha = n / jnp.sum(scaled * scaled)
    x_ref[...] = (2.0 * alpha) * unit - (alpha * alpha) * scaled

    def quick(carry):
        count, unused = carry
        x = x_ref[...]
        rest = unit - rough(scaled_ref[...], x)
        size = jnp.sum(rest * rest)
        x_ref[...] = x + rough(x, rest)
        return (count + 1, size)

    unused, size = lax.while_loop(
        lambda c: (c[0] < QUICK_STEPS) & (c[1] > 0.25), quick, (0, jnp.float32(1e3))
    )

    @pl.when(jnp.logical_not(size <= 0.25))
    def _():
        rows = jnp.sum(jnp.abs(scaled_ref[...]), axis=0, keepdims=True)
        x_ref[...] = unit / jnp.max(rows)

    def sure(carry):
        count, unused = carry
        x = x_ref[...]
        rest = unit - full(scaled_ref[...], x)
        size = jnp.sum(rest * rest)
        x_ref[...] = x + full(x, rest + rough(rest, rest))
        return (count + 1, size)

    lax.while_loop(lambda c: (c[0] < SURE_STEPS) & (c[1] > 3e-4), sure, (0, jnp.float32(1e3)))
    return x_ref[...] * down * along


def invert_pair(pair, scaled_ref, x_ref):
    n = pair[0].shape[0]
    eye = identity(n)
    unit = jnp.where(eye, 1.0, 0.0)
    sides = []
    for k, matrix in enumerate(pair):
        kept = jnp.where(eye, matrix, 0.0)
        along = lax.rsqrt(jnp.sum(kept, axis=0, keepdims=True))
        down = lax.rsqrt(jnp.sum(kept, axis=1, keepdims=True))
        scaled = matrix * down * along
        scaled_ref[k] = scaled
        alpha = n / jnp.sum(scaled * scaled)
        x_ref[k] = (2.0 * alpha) * unit - (alpha * alpha) * scaled
        sides.append((down, along))

    def quick(carry):
        old = [x_ref[k] for k in range(2)]
        rest = [unit - rough(scaled_ref[k], old[k]) for k in range(2)]
        size = [jnp.sum(r * r) for r in rest]
        for k in range(2):
            x_ref[k] = old[k] + rough(old[k], rest[k])
        return (carry[0] + 1, size[0], size[1])

    def below(size, bound):
        return (size[0] <= bound) & (size[1] <= bound)

    start = (0, jnp.float32(1e3), jnp.float32(1e3))
    ended = lax.while_loop(
        lambda c: (c[0] < QUICK_STEPS) & jnp.logical_not(below(c[1:], 0.25)), quick, start
    )
    for k in range(2):

        @pl.when(jnp.logical_not(ended[k + 1] <= 0.25))
        def _():
            rows = jnp.sum(jnp.abs(scaled_ref[k]), axis=0, keepdims=True)
            x_ref[k] = unit / jnp.max(rows)

    def sure(carry):
        old = [x_ref[k] for k in range(2)]
        rest = [unit - full(scaled_ref[k], old[k]) for k in range(2)]
        size = [jnp.sum(r * r) for r in rest]
        more = [r + rough(r, r) for r in rest]
        for k in range(2):
            x_ref[k] = old[k] + full(old[k], more[k])
        return (carry[0] + 1, size[0], size[1])

    lax.while_loop(
        lambda c: (c[0] < SURE_STEPS) & jnp.logical_not(below(c[1:], 3e-4)), sure, start
    )
    return [x_ref[k] * down * along for k, (down, along) in enumerate(sides)]


def combine_into(a_ref, b_ref, out_ref, scaled_ref, x_ref):
    n = b_ref.shape[1]
    inverse = invert(a_ref[2 * n : 3 * n] + b_ref[0:n], scaled_ref, x_ref)
    x_ref[...] = inverse
    left = a_ref[n : 2 * n]
    right = b_ref[n : 2 * n]
    left_x = full(left, x_ref[...])
    x_right = full(x_ref[...], right)
    mid = a_ref[3 * n + 1 : 3 * n + 2] + b_ref[3 * n : 3 * n + 1]
    mid = jnp.broadcast_to(mid, (pad, n))
    out_ref[0:n] = a_ref[0:n] - full(left_x, left, 1, 1)
    out_ref[n : 2 * n] = -full(left_x, right)
    out_ref[2 * n : 3 * n] = b_ref[2 * n : 3 * n] - full(right, x_right, 0, 0)
    row = lax.broadcasted_iota(jnp.int32, (pad, n), 0)
    first = a_ref[3 * n : 3 * n + 1] - full(mid, left_x, 1, 1)
    second = b_ref[3 * n + 1 : 3 * n + 2] - full(mid, x_right)
    out_ref[3 * n : 3 * n + pad] = jnp.where(row == 0, first, jnp.where(row == 1, second, 0.0))


def combine_kernel(flag_ref, a_ref, b_ref, out_ref, scaled_ref, x_ref):
    @pl.when(flag_ref[0] == 0)
    def _():
        out_ref[...] = b_ref[...]

    @pl.when(flag_ref[0] != 0)
    def _():
        combine_into(a_ref, b_ref, out_ref, scaled_ref, x_ref)


def pack_half(core, src, half_ref):
    n = src.shape[1]

    @pl.when(core == 0)
    def _():
        half_ref[0:n] = src[n : 2 * n]
        half_ref[n : n + pad] = src[3 * n : 3 * n + pad]

    @pl.when(core != 0)
    def _():
        down = lax.broadcasted_iota(jnp.int32, (n, n), 0)
        along = lax.broadcasted_iota(jnp.int32, (n, n), 1)
        out = src[2 * n : 3 * n]
        half_ref[0:n] = jnp.where(down <= along, src[0:n], out)
        diagonal = jnp.sum(jnp.where(down == along, out, 0.0), axis=0, keepdims=True)
        row = lax.broadcasted_iota(jnp.int32, (pad, n), 0)
        half_ref[n : n + pad] = jnp.where(row == 2, diagonal, src[3 * n : 3 * n + pad])


def unpack(cross_ref, both_ref, dst):
    n = dst.shape[1]
    down = lax.broadcasted_iota(jnp.int32, (n, n), 0)
    along = lax.broadcasted_iota(jnp.int32, (n, n), 1)
    both = both_ref[0:n]
    flipped = both.T
    dst[0:n] = jnp.where(down <= along, both, flipped)
    dst[n : 2 * n] = cross_ref[0:n]
    out = jnp.where(down > along, both, flipped)
    dst[2 * n : 3 * n] = jnp.where(down == along, both_ref[n + 2 : n + 3], out)
    row = lax.broadcasted_iota(jnp.int32, (pad, n), 0)
    dst[3 * n : 3 * n + pad] = jnp.where(row < 2, both_ref[n : n + pad], 0.0)


def chip_kernel(core_ref, own_ref, other_ref, total_ref, half_ref, scaled_ref, x_ref):
    core = core_ref[0]

    @pl.when(core == 0)
    def _():
        combine_into(own_ref, other_ref, total_ref, scaled_ref, x_ref)

    @pl.when(core != 0)
    def _():
        combine_into(other_ref, own_ref, total_ref, scaled_ref, x_ref)

    pack_half(core, total_ref, half_ref)


def advance_into(a_ref, b_ref, out_ref, scaled_ref, x_ref):
    n = b_ref.shape[1]
    inverse = invert(a_ref[0:n] + b_ref[0:n], scaled_ref, x_ref)
    right = b_ref[n : 2 * n]
    x_right = full(inverse, right)
    mid = a_ref[n + 1 : n + 2] + b_ref[3 * n : 3 * n + 1]
    mid = jnp.broadcast_to(mid, (pad, n))
    out_ref[0:n] = b_ref[2 * n : 3 * n] - full(right, x_right, 0, 0)
    second = b_ref[3 * n + 1 : 3 * n + 2] - full(mid, x_right)
    row = lax.broadcasted_iota(jnp.int32, (pad, n), 0)
    out_ref[n : n + pad] = jnp.where(row == 1, second, 0.0)


def plane_kernel(
    place_ref, mine_ref, theirs_ref, own_ref, group_ref, chip_ref, state_ref, scaled_ref, x_ref
):
    n = own_ref.shape[1]

    @pl.when(place_ref[0] == 0)
    def _():
        unpack(mine_ref, theirs_ref, chip_ref)

    @pl.when(place_ref[0] != 0)
    def _():
        unpack(theirs_ref, mine_ref, chip_ref)

    @pl.when(place_ref[1] == 0)
    def _():
        combine_into(own_ref, chip_ref, group_ref, scaled_ref, x_ref)

    @pl.when(place_ref[1] != 0)
    def _():
        combine_into(chip_ref, own_ref, group_ref, scaled_ref, x_ref)

    state_ref[...] = group_ref[2 * n : 3 * n + pad]


def advance_kernel(flag_ref, a_ref, b_ref, out_ref, scaled_ref, x_ref):
    @pl.when(flag_ref[0] == 0)
    def _():
        n = b_ref.shape[1]
        out_ref[...] = b_ref[2 * n : 3 * n + pad]

    @pl.when(flag_ref[0] != 0)
    def _():
        advance_into(a_ref, b_ref, out_ref, scaled_ref, x_ref)


def last_kernel(flag_ref, a_ref, b_ref, c_ref, cov_ref, mean_ref, s_ref, scaled_ref, x_ref):
    n = a_ref.shape[1]
    both = (b_ref, c_ref)

    @pl.when(flag_ref[0] == 0)
    def _():
        for k, e_ref in enumerate(both):
            s_ref[k] = e_ref[2 * n : 3 * n + pad]

    @pl.when(flag_ref[0] != 0)
    def _():
        inverses = invert_pair([a_ref[0:n] + e_ref[0:n] for e_ref in both], scaled_ref, x_ref)
        row = lax.broadcasted_iota(jnp.int32, (pad, n), 0)
        for k, e_ref in enumerate(both):
            right = e_ref[n : 2 * n]
            x_right = full(inverses[k], right)
            mid = a_ref[n + 1 : n + 2] + e_ref[3 * n : 3 * n + 1]
            mid = jnp.broadcast_to(mid, (pad, n))
            s_ref[k, 0:n] = e_ref[2 * n : 3 * n] - full(right, x_right, 0, 0)
            second = e_ref[3 * n + 1 : 3 * n + 2] - full(mid, x_right)
            s_ref[k, n : n + pad] = jnp.where(row == 1, second, 0.0)

    covs = invert_pair([s_ref[k, 0:n] for k in range(2)], scaled_ref, x_ref)
    for k in range(2):
        cov_ref[k] = covs[k]
        mean_ref[k] = full(s_ref[k, n : n + pad], covs[k], 1, 1)


vmem = pl.BlockSpec(memory_space=pltpu.VMEM)
smem = pl.BlockSpec(memory_space=pltpu.SMEM)


def call(kernel, specs, shapes, n, *extra, wide=()):
    return pl.pallas_call(
        kernel,
        out_shape=shapes,
        in_specs=specs,
        out_specs=jax.tree.map(lambda unused: vmem, shapes),
        scratch_shapes=[*extra] + [pltpu.VMEM((*wide, n, n), jnp.float32)] * 2,
        compiler_params=pltpu.CompilerParams(vmem_limit_bytes=40 * 1024 * 1024),
        cost_estimate=pl.CostEstimate(flops=20_000_000_000, bytes_accessed=3_000_000, transcendentals=0),
    )


def f32(*shape):
    return jax.ShapeDtypeStruct(shape, jnp.float32)


def combine(flag, earlier, later):
    n = later.shape[1]
    return call(combine_kernel, [smem, vmem, vmem], f32(3 * n + pad, n), n)(flag, earlier, later)


def advance(flag, earlier, later):
    n = later.shape[1]
    return call(advance_kernel, [smem, vmem, vmem], f32(n + pad, n), n)(flag, earlier, later)


def chip_total(core, own, other):
    n = own.shape[1]
    shapes = (f32(3 * n + pad, n), f32(n + pad, n))
    return call(chip_kernel, [smem, vmem, vmem], shapes, n)(core, own, other)


def plane_total(place, mine, theirs, own):
    n = own.shape[1]
    shapes = (f32(3 * n + pad, n), f32(3 * n + pad, n), f32(n + pad, n))
    return call(plane_kernel, [smem, vmem, vmem, vmem], shapes, n)(place, mine, theirs, own)


def filtered(flag, earlier, first, second):
    n = earlier.shape[1]
    return call(
        last_kernel,
        [smem, vmem, vmem, vmem],
        (f32(2, n, n), f32(2, pad, n)),
        n,
        pltpu.VMEM((2, n + pad, n), jnp.float32),
        wide=(2,),
    )(flag, earlier, first, second)


def gram_kernel(x_ref, out_ref):
    peers, n = x_ref.shape[1], x_ref.shape[4]
    sensors = x_ref.shape[3] - extra
    half = n // 2
    rows = x_ref[0, :, 0, 0:sensors, :].reshape(peers * sensors, n)
    gram = lax.dot_general(
        rows, rows, (((0,), (0,)), ((), ())), preferred_element_type=jnp.float32
    )
    out_ref[0, 0, 0:half] = gram[0:half]
    out_ref[0, 0, half : half + half // 2, 0:half] = gram[half : half + half // 2, half:]
    out_ref[0, 0, half : half + half // 2, half:] = gram[half + half // 2 :, half:]
    tail = x_ref[0, :, 0, sensors:, :].astype(jnp.float32).reshape(peers * extra, n)
    info = jnp.sum(tail, axis=0, keepdims=True)
    out_ref[0, 0, half + half // 2 :] = jnp.broadcast_to(info, (pad, n))


def gram_terms(rows):
    blocks, peers, steps, height, n = rows.shape
    tall = n // 2 + n // 4 + pad
    return pl.pallas_call(
        gram_kernel,
        grid=(blocks, steps),
        out_shape=f32(blocks, steps, tall, n),
        in_specs=[pl.BlockSpec((1, peers, 1, height, n), lambda i, j: (i, 0, j, 0, 0))],
        out_specs=pl.BlockSpec((1, 1, tall, n), lambda i, j: (i, j, 0, 0)),
        compiler_params=pltpu.CompilerParams(vmem_limit_bytes=24 * 1024 * 1024),
    )(rows)


def whole_gram(packed):
    n = packed.shape[1]
    half, quarter = n // 2, n // 4
    low = packed[half : half + quarter]
    corner = jnp.concatenate([low[:, :half], low[:, half:]], axis=0)
    top = packed[:half]
    return jnp.concatenate([top, jnp.concatenate([top[:, half:].T, corner], axis=1)], axis=0)


def three_terms(x):
    high = lax.reduce_precision(x, 8, 7)
    rest = x - high
    middle = lax.reduce_precision(rest, 8, 7)
    return jnp.stack([high, middle, rest - middle], axis=1).astype(jnp.bfloat16)


def swap(x, axis):
    return lax.ppermute(x, axis, [(0, 1), (1, 0)])


def flag(*values):
    return jnp.stack([jnp.asarray(value, jnp.int32) for value in values])


def body(obs_rows, readings, available, sensor_ids, noise_var, col_scale, transition, process_info):
    n = obs_rows.shape[2]
    sensor_total = noise_var.shape[0]
    lookup_table = (
        sensor_ids[:, None] == jnp.arange(sensor_total, dtype=jnp.int32)[None, :]
    ).astype(jnp.float32)
    local_var = matmul(lookup_table, noise_var)
    weight = available.astype(jnp.float32) * lax.rsqrt(local_var)[None, :]
    weighted = (obs_rows.astype(jnp.float32) * weight[:, :, None]).astype(jnp.bfloat16)
    signal = (readings * weight).astype(jnp.bfloat16)
    own_info = jnp.einsum("tm,tms->ts", signal, weighted, preferred_element_type=jnp.float32)
    steps = obs_rows.shape[0]
    planes, plane_size = lax.axis_size("tm"), lax.axis_size(("sensor", "state"))
    block_len = steps // (planes * plane_size)
    terms = three_terms(own_info)
    terms = jnp.pad(terms, ((0, 0), (0, extra - terms.shape[1]), (0, 0)))
    sent = jnp.concatenate([weighted, terms], axis=1)
    sent = sent.reshape(planes, plane_size, block_len, sent.shape[1], n)
    packed = []
    for k in range(block_len):
        arrived = lax.all_to_all(
            sent[:, :, k : k + 1], ("sensor", "state"), split_axis=1, concat_axis=1, tiled=True
        )
        packed.append(
            lax.psum_scatter(gram_terms(arrived), "tm", scatter_dimension=0, tiled=True)[0, 0]
        )
    gram_part = [whole_gram(packed[k]) for k in range(block_len)]
    info_part = [part[n // 2 + n // 4] for part in packed]
    mine = lax.axis_index(everyone)
    carried = matmul(process_info, transition)
    inward = matmul(transition.T, carried)
    outer_scale = col_scale[:, None] * col_scale[None, :]

    def element(k):
        keep = (mine * block_len + k > 0).astype(jnp.float32)
        vectors = jnp.concatenate(
            [
                jnp.zeros((1, n), jnp.float32),
                (info_part[k] * col_scale)[None, :],
                jnp.zeros((pad - 2, n), jnp.float32),
            ]
        )
        return jnp.concatenate(
            [
                inward * keep,
                carried.T * -keep,
                process_info + gram_part[k] * outer_scale,
                vectors,
            ]
        )

    elements = [element(k) for k in range(block_len)]
    summary = combine(flag(1), elements[0], elements[1])

    core = lax.axis_index("state")
    chips, chip = lax.axis_size("sensor"), lax.axis_index("sensor")
    planes, plane = lax.axis_size("tm"), lax.axis_index("tm")
    other = swap(summary, "state")
    own_chip, half = chip_total(flag(core), summary, other)
    if chips == 2:
        mine_half = swap(half, "sensor")
        theirs_half = swap(mine_half, "state")
        group, prior, state = plane_total(flag(core, chip), mine_half, theirs_half, own_chip)
        has_prior = chip > 0
    else:
        everything = lax.all_gather(own_chip, "sensor")
        group, prior = everything[0], everything[0]
        for k in range(1, chips):
            group = combine(flag(1), group, everything[k])
            if k < chips - 1:
                prior = jnp.where(k < chip, group, prior)
        has_prior = chip > 0
        state = group[2 * n :]

    incoming = jnp.zeros_like(state)
    for k in range(1, planes):
        perm = [(k - 1, k)]
        came = lax.ppermute(state, "tm", perm)
        if k < planes - 1:
            state = advance(flag(plane == k), came, group)
        incoming = incoming + came

    ahead = combine(flag(has_prior & (core > 0)), prior, other)
    ahead = jnp.where(core > 0, ahead, prior)
    has_ahead = has_prior | (core > 0)
    first = combine(flag(has_ahead), ahead, elements[0])
    second = combine(flag(has_ahead), ahead, summary)
    covs, means = filtered(flag(plane > 0), incoming, first, second)
    return (means[:, 1], covs)


def solution(mesh):
    in_specs = (
        P("groups", ("tm", "sensor", "state"), None),
        P("groups", ("tm", "sensor", "state")),
        P("groups", ("tm", "sensor", "state")),
        P(("groups", "tm", "sensor", "state")),
        P(),
        P(),
        P(),
        P(),
    )
    out_specs = (
        P(("groups", "tm", "sensor", "state"), None),
        P(("groups", "tm", "sensor", "state"), None, None),
    )
    return jax.shard_map(body, mesh=mesh, in_specs=in_specs, out_specs=out_specs, check_vma=False)
```

```python
import jax
import jax.numpy as jnp
from jax import lax
from jax.experimental import pallas as pl
from jax.experimental.pallas import tpu as pltpu
from jax.sharding import PartitionSpec as P

highest = lax.Precision.HIGHEST
everyone = ("tm", "sensor", "state")
pad = 8
extra = 16

QUICK_STEPS = 12
SURE_STEPS = 48


def matmul(first_op, second_op):
    return jnp.dot(first_op, second_op, precision=highest)


def full(a, b, ca=1, cb=0):
    return lax.dot_general(
        a, b, (((ca,), (cb,)), ((), ())), precision=highest, preferred_element_type=jnp.float32
    )


def rough(a, b):
    return jnp.dot(
        a.astype(jnp.bfloat16), b.astype(jnp.bfloat16), preferred_element_type=jnp.float32
    )


def identity(n):
    return lax.broadcasted_iota(jnp.int32, (n, n), 0) == lax.broadcasted_iota(
        jnp.int32, (n, n), 1
    )


def invert(matrix, scaled_ref, x_ref):
    n = matrix.shape[0]
    eye = identity(n)
    unit = jnp.where(eye, 1.0, 0.0)
    kept = jnp.where(eye, matrix, 0.0)
    along = lax.rsqrt(jnp.sum(kept, axis=0, keepdims=True))
    down = lax.rsqrt(jnp.sum(kept, axis=1, keepdims=True))
    scaled = matrix * down * along
    scaled_ref[...] = scaled
    alpha = 2.0 / (1.0 + jnp.max(jnp.sum(jnp.abs(scaled), axis=0, keepdims=True)))
    x_ref[...] = (2.0 * alpha) * unit - (alpha * alpha) * scaled

    def quick(carry):
        count, unused = carry
        x = x_ref[...]
        rest = unit - rough(scaled_ref[...], x)
        size = jnp.sum(rest * rest)
        x_ref[...] = x + rough(x, rest)
        return (count + 1, size)

    unused, size = lax.while_loop(
        lambda c: (c[0] < QUICK_STEPS) & (c[1] > 0.25), quick, (0, jnp.float32(1e3))
    )

    @pl.when(jnp.logical_not(size <= 0.8))
    def _():
        rows = jnp.sum(jnp.abs(scaled_ref[...]), axis=0, keepdims=True)
        x_ref[...] = unit / jnp.max(rows)

    def sure(carry):
        count, unused = carry
        x = x_ref[...]
        rest = unit - full(scaled_ref[...], x)
        size = jnp.sum(rest * rest)
        x_ref[...] = x + full(x, rest + rough(rest, rest))
        return (count + 1, size)

    lax.while_loop(lambda c: (c[0] < SURE_STEPS) & (c[1] > 3e-4), sure, (0, jnp.float32(1e3)))
    return x_ref[...] * down * along


def invert_pair(pair, scaled_ref, x_ref):
    n = pair[0].shape[0]
    eye = identity(n)
    unit = jnp.where(eye, 1.0, 0.0)
    sides = []
    for k, matrix in enumerate(pair):
        kept = jnp.where(eye, matrix, 0.0)
        along = lax.rsqrt(jnp.sum(kept, axis=0, keepdims=True))
        down = lax.rsqrt(jnp.sum(kept, axis=1, keepdims=True))
        scaled = matrix * down * along
        scaled_ref[k] = scaled
        alpha = 2.0 / (1.0 + jnp.max(jnp.sum(jnp.abs(scaled), axis=0, keepdims=True)))
        x_ref[k] = (2.0 * alpha) * unit - (alpha * alpha) * scaled
        sides.append((down, along))

    def quick(carry):
        old = [x_ref[k] for k in range(2)]
        rest = [unit - rough(scaled_ref[k], old[k]) for k in range(2)]
        size = [jnp.sum(r * r) for r in rest]
        for k in range(2):
            x_ref[k] = old[k] + rough(old[k], rest[k])
        return (carry[0] + 1, size[0], size[1])

    def below(size, bound):
        return (size[0] <= bound) & (size[1] <= bound)

    start = (0, jnp.float32(1e3), jnp.float32(1e3))
    ended = lax.while_loop(
        lambda c: (c[0] < QUICK_STEPS) & jnp.logical_not(below(c[1:], 0.25)), quick, start
    )
    for k in range(2):

        @pl.when(jnp.logical_not(ended[k + 1] <= 0.8))
        def _():
            rows = jnp.sum(jnp.abs(scaled_ref[k]), axis=0, keepdims=True)
            x_ref[k] = unit / jnp.max(rows)

    def sure(carry):
        old = [x_ref[k] for k in range(2)]
        rest = [unit - full(scaled_ref[k], old[k]) for k in range(2)]
        size = [jnp.sum(r * r) for r in rest]
        more = [r + rough(r, r) for r in rest]
        for k in range(2):
            x_ref[k] = old[k] + full(old[k], more[k])
        return (carry[0] + 1, size[0], size[1])

    lax.while_loop(
        lambda c: (c[0] < SURE_STEPS) & jnp.logical_not(below(c[1:], 3e-4)), sure, start
    )
    return [x_ref[k] * down * along for k, (down, along) in enumerate(sides)]


def combine_into(a_ref, b_ref, out_ref, scaled_ref, x_ref):
    n = b_ref.shape[1]
    inverse = invert(a_ref[2 * n : 3 * n] + b_ref[0:n], scaled_ref, x_ref)
    x_ref[...] = inverse
    left = a_ref[n : 2 * n]
    right = b_ref[n : 2 * n]
    left_x = full(left, x_ref[...])
    x_right = full(x_ref[...], right)
    mid = a_ref[3 * n + 1 : 3 * n + 2] + b_ref[3 * n : 3 * n + 1]
    mid = jnp.broadcast_to(mid, (pad, n))
    out_ref[0:n] = a_ref[0:n] - full(left_x, left, 1, 1)
    out_ref[n : 2 * n] = -full(left_x, right)
    out_ref[2 * n : 3 * n] = b_ref[2 * n : 3 * n] - full(right, x_right, 0, 0)
    row = lax.broadcasted_iota(jnp.int32, (pad, n), 0)
    first = a_ref[3 * n : 3 * n + 1] - full(mid, left_x, 1, 1)
    second = b_ref[3 * n + 1 : 3 * n + 2] - full(mid, x_right)
    out_ref[3 * n : 3 * n + pad] = jnp.where(row == 0, first, jnp.where(row == 1, second, 0.0))


def combine_kernel(flag_ref, a_ref, b_ref, out_ref, scaled_ref, x_ref):
    @pl.when(flag_ref[0] == 0)
    def _():
        out_ref[...] = b_ref[...]

    @pl.when(flag_ref[0] != 0)
    def _():
        combine_into(a_ref, b_ref, out_ref, scaled_ref, x_ref)


def pack_half(core, src, half_ref):
    n = src.shape[1]

    @pl.when(core == 0)
    def _():
        half_ref[0:n] = src[n : 2 * n]
        half_ref[n : n + pad] = src[3 * n : 3 * n + pad]

    @pl.when(core != 0)
    def _():
        down = lax.broadcasted_iota(jnp.int32, (n, n), 0)
        along = lax.broadcasted_iota(jnp.int32, (n, n), 1)
        out = src[2 * n : 3 * n]
        half_ref[0:n] = jnp.where(down <= along, src[0:n], out)
        diagonal = jnp.sum(jnp.where(down == along, out, 0.0), axis=0, keepdims=True)
        row = lax.broadcasted_iota(jnp.int32, (pad, n), 0)
        half_ref[n : n + pad] = jnp.where(row == 2, diagonal, src[3 * n : 3 * n + pad])


def unpack(cross_ref, both_ref, dst):
    n = dst.shape[1]
    down = lax.broadcasted_iota(jnp.int32, (n, n), 0)
    along = lax.broadcasted_iota(jnp.int32, (n, n), 1)
    both = both_ref[0:n]
    flipped = both.T
    dst[0:n] = jnp.where(down <= along, both, flipped)
    dst[n : 2 * n] = cross_ref[0:n]
    out = jnp.where(down > along, both, flipped)
    dst[2 * n : 3 * n] = jnp.where(down == along, both_ref[n + 2 : n + 3], out)
    row = lax.broadcasted_iota(jnp.int32, (pad, n), 0)
    dst[3 * n : 3 * n + pad] = jnp.where(row < 2, both_ref[n : n + pad], 0.0)


def chip_kernel(core_ref, own_ref, other_ref, total_ref, half_ref, scaled_ref, x_ref):
    core = core_ref[0]

    @pl.when(core == 0)
    def _():
        combine_into(own_ref, other_ref, total_ref, scaled_ref, x_ref)

    @pl.when(core != 0)
    def _():
        combine_into(other_ref, own_ref, total_ref, scaled_ref, x_ref)

    pack_half(core, total_ref, half_ref)


def advance_into(a_ref, b_ref, out_ref, scaled_ref, x_ref):
    n = b_ref.shape[1]
    inverse = invert(a_ref[0:n] + b_ref[0:n], scaled_ref, x_ref)
    right = b_ref[n : 2 * n]
    x_right = full(inverse, right)
    mid = a_ref[n + 1 : n + 2] + b_ref[3 * n : 3 * n + 1]
    mid = jnp.broadcast_to(mid, (pad, n))
    out_ref[0:n] = b_ref[2 * n : 3 * n] - full(right, x_right, 0, 0)
    second = b_ref[3 * n + 1 : 3 * n + 2] - full(mid, x_right)
    row = lax.broadcasted_iota(jnp.int32, (pad, n), 0)
    out_ref[n : n + pad] = jnp.where(row == 1, second, 0.0)


def plane_kernel(
    place_ref, mine_ref, theirs_ref, own_ref, group_ref, chip_ref, state_ref, scaled_ref, x_ref
):
    n = own_ref.shape[1]

    @pl.when(place_ref[0] == 0)
    def _():
        unpack(mine_ref, theirs_ref, chip_ref)

    @pl.when(place_ref[0] != 0)
    def _():
        unpack(theirs_ref, mine_ref, chip_ref)

    @pl.when(place_ref[1] == 0)
    def _():
        combine_into(own_ref, chip_ref, group_ref, scaled_ref, x_ref)

    @pl.when(place_ref[1] != 0)
    def _():
        combine_into(chip_ref, own_ref, group_ref, scaled_ref, x_ref)

    state_ref[...] = group_ref[2 * n : 3 * n + pad]


def advance_kernel(flag_ref, a_ref, b_ref, out_ref, scaled_ref, x_ref):
    @pl.when(flag_ref[0] == 0)
    def _():
        n = b_ref.shape[1]
        out_ref[...] = b_ref[2 * n : 3 * n + pad]

    @pl.when(flag_ref[0] != 0)
    def _():
        advance_into(a_ref, b_ref, out_ref, scaled_ref, x_ref)


def last_kernel(flag_ref, a_ref, b_ref, c_ref, cov_ref, mean_ref, s_ref, scaled_ref, x_ref):
    n = a_ref.shape[1]
    both = (b_ref, c_ref)

    @pl.when(flag_ref[0] == 0)
    def _():
        for k, e_ref in enumerate(both):
            s_ref[k] = e_ref[2 * n : 3 * n + pad]

    @pl.when(flag_ref[0] != 0)
    def _():
        inverses = invert_pair([a_ref[0:n] + e_ref[0:n] for e_ref in both], scaled_ref, x_ref)
        row = lax.broadcasted_iota(jnp.int32, (pad, n), 0)
        for k, e_ref in enumerate(both):
            right = e_ref[n : 2 * n]
            x_right = full(inverses[k], right)
            mid = a_ref[n + 1 : n + 2] + e_ref[3 * n : 3 * n + 1]
            mid = jnp.broadcast_to(mid, (pad, n))
            s_ref[k, 0:n] = e_ref[2 * n : 3 * n] - full(right, x_right, 0, 0)
            second = e_ref[3 * n + 1 : 3 * n + 2] - full(mid, x_right)
            s_ref[k, n : n + pad] = jnp.where(row == 1, second, 0.0)

    covs = invert_pair([s_ref[k, 0:n] for k in range(2)], scaled_ref, x_ref)
    for k in range(2):
        cov_ref[k] = covs[k]
        mean_ref[k] = full(s_ref[k, n : n + pad], covs[k], 1, 1)


vmem = pl.BlockSpec(memory_space=pltpu.VMEM)
smem = pl.BlockSpec(memory_space=pltpu.SMEM)


def call(kernel, specs, shapes, n, *extra, wide=()):
    return pl.pallas_call(
        kernel,
        out_shape=shapes,
        in_specs=specs,
        out_specs=jax.tree.map(lambda unused: vmem, shapes),
        scratch_shapes=[*extra] + [pltpu.VMEM((*wide, n, n), jnp.float32)] * 2,
        compiler_params=pltpu.CompilerParams(vmem_limit_bytes=40 * 1024 * 1024),
        cost_estimate=pl.CostEstimate(flops=20_000_000_000, bytes_accessed=3_000_000, transcendentals=0),
    )


def f32(*shape):
    return jax.ShapeDtypeStruct(shape, jnp.float32)


def combine(flag, earlier, later):
    n = later.shape[1]
    return call(combine_kernel, [smem, vmem, vmem], f32(3 * n + pad, n), n)(flag, earlier, later)


def advance(flag, earlier, later):
    n = later.shape[1]
    return call(advance_kernel, [smem, vmem, vmem], f32(n + pad, n), n)(flag, earlier, later)


def chip_total(core, own, other):
    n = own.shape[1]
    shapes = (f32(3 * n + pad, n), f32(n + pad, n))
    return call(chip_kernel, [smem, vmem, vmem], shapes, n)(core, own, other)


def plane_total(place, mine, theirs, own):
    n = own.shape[1]
    shapes = (f32(3 * n + pad, n), f32(3 * n + pad, n), f32(n + pad, n))
    return call(plane_kernel, [smem, vmem, vmem, vmem], shapes, n)(place, mine, theirs, own)


def filtered(flag, earlier, first, second):
    n = earlier.shape[1]
    return call(
        last_kernel,
        [smem, vmem, vmem, vmem],
        (f32(2, n, n), f32(2, pad, n)),
        n,
        pltpu.VMEM((2, n + pad, n), jnp.float32),
        wide=(2,),
    )(flag, earlier, first, second)


def gram_kernel(x_ref, out_ref):
    peers, n = x_ref.shape[1], x_ref.shape[4]
    sensors = x_ref.shape[3] - extra
    half = n // 2
    rows = x_ref[0, :, 0, 0:sensors, :].reshape(peers * sensors, n)
    gram = lax.dot_general(
        rows, rows, (((0,), (0,)), ((), ())), preferred_element_type=jnp.float32
    )
    out_ref[0, 0, 0:half] = gram[0:half]
    out_ref[0, 0, half : half + half // 2, 0:half] = gram[half : half + half // 2, half:]
    out_ref[0, 0, half : half + half // 2, half:] = gram[half + half // 2 :, half:]
    tail = x_ref[0, :, 0, sensors:, :].astype(jnp.float32).reshape(peers * extra, n)
    info = jnp.sum(tail, axis=0, keepdims=True)
    out_ref[0, 0, half + half // 2 :] = jnp.broadcast_to(info, (pad, n))


def gram_terms(rows):
    blocks, peers, steps, height, n = rows.shape
    tall = n // 2 + n // 4 + pad
    return pl.pallas_call(
        gram_kernel,
        grid=(blocks, steps),
        out_shape=f32(blocks, steps, tall, n),
        in_specs=[pl.BlockSpec((1, peers, 1, height, n), lambda i, j: (i, 0, j, 0, 0))],
        out_specs=pl.BlockSpec((1, 1, tall, n), lambda i, j: (i, j, 0, 0)),
        compiler_params=pltpu.CompilerParams(vmem_limit_bytes=24 * 1024 * 1024),
    )(rows)


def whole_gram(packed):
    n = packed.shape[1]
    half, quarter = n // 2, n // 4
    low = packed[half : half + quarter]
    corner = jnp.concatenate([low[:, :half], low[:, half:]], axis=0)
    top = packed[:half]
    return jnp.concatenate([top, jnp.concatenate([top[:, half:].T, corner], axis=1)], axis=0)


def three_terms(x):
    high = lax.reduce_precision(x, 8, 7)
    rest = x - high
    middle = lax.reduce_precision(rest, 8, 7)
    return jnp.stack([high, middle, rest - middle], axis=1).astype(jnp.bfloat16)


def swap(x, axis):
    return lax.ppermute(x, axis, [(0, 1), (1, 0)])


def flag(*values):
    return jnp.stack([jnp.asarray(value, jnp.int32) for value in values])


def body(obs_rows, readings, available, sensor_ids, noise_var, col_scale, transition, process_info):
    n = obs_rows.shape[2]
    sensor_total = noise_var.shape[0]
    lookup_table = (
        sensor_ids[:, None] == jnp.arange(sensor_total, dtype=jnp.int32)[None, :]
    ).astype(jnp.float32)
    local_var = matmul(lookup_table, noise_var)
    weight = available.astype(jnp.float32) * lax.rsqrt(local_var)[None, :]
    weighted = (obs_rows.astype(jnp.float32) * weight[:, :, None]).astype(jnp.bfloat16)
    signal = (readings * weight).astype(jnp.bfloat16)
    own_info = jnp.einsum("tm,tms->ts", signal, weighted, preferred_element_type=jnp.float32)
    steps = obs_rows.shape[0]
    planes, plane_size = lax.axis_size("tm"), lax.axis_size(("sensor", "state"))
    block_len = steps // (planes * plane_size)
    terms = three_terms(own_info)
    terms = jnp.pad(terms, ((0, 0), (0, extra - terms.shape[1]), (0, 0)))
    sent = jnp.concatenate([weighted, terms], axis=1)
    sent = sent.reshape(planes, plane_size, block_len, sent.shape[1], n)
    packed = []
    for k in range(block_len):
        arrived = lax.all_to_all(
            sent[:, :, k : k + 1], ("sensor", "state"), split_axis=1, concat_axis=1, tiled=True
        )
        packed.append(
            lax.psum_scatter(gram_terms(arrived), "tm", scatter_dimension=0, tiled=True)[0, 0]
        )
    gram_part = [whole_gram(packed[k]) for k in range(block_len)]
    info_part = [part[n // 2 + n // 4] for part in packed]
    mine = lax.axis_index(everyone)
    carried = matmul(process_info, transition)
    inward = matmul(transition.T, carried)
    outer_scale = col_scale[:, None] * col_scale[None, :]

    def element(k):
        keep = (mine * block_len + k > 0).astype(jnp.float32)
        vectors = jnp.concatenate(
            [
                jnp.zeros((1, n), jnp.float32),
                (info_part[k] * col_scale)[None, :],
                jnp.zeros((pad - 2, n), jnp.float32),
            ]
        )
        return jnp.concatenate(
            [
                inward * keep,
                carried.T * -keep,
                process_info + gram_part[k] * outer_scale,
                vectors,
            ]
        )

    elements = [element(k) for k in range(block_len)]
    summary = combine(flag(1), elements[0], elements[1])

    core = lax.axis_index("state")
    chips, chip = lax.axis_size("sensor"), lax.axis_index("sensor")
    planes, plane = lax.axis_size("tm"), lax.axis_index("tm")
    other = swap(summary, "state")
    own_chip, half = chip_total(flag(core), summary, other)
    if chips == 2:
        mine_half = swap(half, "sensor")
        theirs_half = swap(mine_half, "state")
        group, prior, state = plane_total(flag(core, chip), mine_half, theirs_half, own_chip)
        has_prior = chip > 0
    else:
        everything = lax.all_gather(own_chip, "sensor")
        group, prior = everything[0], everything[0]
        for k in range(1, chips):
            group = combine(flag(1), group, everything[k])
            if k < chips - 1:
                prior = jnp.where(k < chip, group, prior)
        has_prior = chip > 0
        state = group[2 * n :]

    incoming = jnp.zeros_like(state)
    for k in range(1, planes):
        perm = [(k - 1, k)]
        came = lax.ppermute(state, "tm", perm)
        if k < planes - 1:
            state = advance(flag(plane == k), came, group)
        incoming = incoming + came

    ahead = combine(flag(has_prior & (core > 0)), prior, other)
    ahead = jnp.where(core > 0, ahead, prior)
    has_ahead = has_prior | (core > 0)
    first = combine(flag(has_ahead), ahead, elements[0])
    second = combine(flag(has_ahead), ahead, summary)
    covs, means = filtered(flag(plane > 0), incoming, first, second)
    return (means[:, 1], covs)


def solution(mesh):
    in_specs = (
        P("groups", ("tm", "sensor", "state"), None),
        P("groups", ("tm", "sensor", "state")),
        P("groups", ("tm", "sensor", "state")),
        P(("groups", "tm", "sensor", "state")),
        P(),
        P(),
        P(),
        P(),
    )
    out_specs = (
        P(("groups", "tm", "sensor", "state"), None),
        P(("groups", "tm", "sensor", "state"), None, None),
    )
    return jax.shard_map(body, mesh=mesh, in_specs=in_specs, out_specs=out_specs, check_vma=False)
```

```python
import jax
import jax.numpy as jnp
from jax import lax
from jax.experimental import pallas as pl
from jax.experimental.pallas import tpu as pltpu
from jax.sharding import PartitionSpec as P

highest = lax.Precision.HIGHEST
everyone = ("tm", "sensor", "state")
pad = 8
extra = 16

QUICK_STEPS = 8
SURE_STEPS = 48


def matmul(first_op, second_op):
    return jnp.dot(first_op, second_op, precision=highest)


def full(a, b, ca=1, cb=0):
    return lax.dot_general(
        a, b, (((ca,), (cb,)), ((), ())), precision=highest, preferred_element_type=jnp.float32
    )


def rough(a, b):
    return jnp.dot(
        a.astype(jnp.bfloat16), b.astype(jnp.bfloat16), preferred_element_type=jnp.float32
    )


def identity(n):
    return lax.broadcasted_iota(jnp.int32, (n, n), 0) == lax.broadcasted_iota(
        jnp.int32, (n, n), 1
    )


def invert(matrix, scaled_ref, x_ref):
    n = matrix.shape[0]
    eye = identity(n)
    unit = jnp.where(eye, 1.0, 0.0)
    kept = jnp.where(eye, matrix, 0.0)
    along = lax.rsqrt(jnp.sum(kept, axis=0, keepdims=True))
    down = lax.rsqrt(jnp.sum(kept, axis=1, keepdims=True))
    scaled = matrix * down * along
    scaled_ref[...] = scaled
    alpha = n / jnp.sum(scaled * scaled)
    x_ref[...] = (2.0 * alpha) * unit - (alpha * alpha) * scaled

    def quick(carry):
        count, unused = carry
        x = x_ref[...]
        rest = unit - rough(scaled_ref[...], x)
        size = jnp.sum(rest * rest)
        x_ref[...] = x + rough(x, rest)
        return (count + 1, size)

    lax.while_loop(
        lambda c: (c[0] < QUICK_STEPS) & (c[1] > 0.25), quick, (0, jnp.float32(1e3))
    )

    def sure(carry):
        count, unused = carry
        x = x_ref[...]
        rest = unit - full(scaled_ref[...], x)
        size = jnp.sum(rest * rest)
        x_ref[...] = x + full(x, rest + rough(rest, rest))

        @pl.when(jnp.logical_not(size <= n))
        def _():
            rows = jnp.sum(jnp.abs(scaled_ref[...]), axis=0, keepdims=True)
            x_ref[...] = unit / jnp.max(rows)

        return (count + 1, jnp.where(size <= n, size, 1e3))

    lax.while_loop(lambda c: (c[0] < SURE_STEPS) & (c[1] > 3e-4), sure, (0, jnp.float32(1e3)))
    return x_ref[...] * down * along


def invert_pair(pair, scaled_ref, x_ref):
    n = pair[0].shape[0]
    eye = identity(n)
    unit = jnp.where(eye, 1.0, 0.0)
    sides = []
    for k, matrix in enumerate(pair):
        kept = jnp.where(eye, matrix, 0.0)
        along = lax.rsqrt(jnp.sum(kept, axis=0, keepdims=True))
        down = lax.rsqrt(jnp.sum(kept, axis=1, keepdims=True))
        scaled = matrix * down * along
        scaled_ref[k] = scaled
        alpha = n / jnp.sum(scaled * scaled)
        x_ref[k] = (2.0 * alpha) * unit - (alpha * alpha) * scaled
        sides.append((down, along))

    def quick(carry):
        old = [x_ref[k] for k in range(2)]
        rest = [unit - rough(scaled_ref[k], old[k]) for k in range(2)]
        size = [jnp.sum(r * r) for r in rest]
        for k in range(2):
            x_ref[k] = old[k] + rough(old[k], rest[k])
        return (carry[0] + 1, size[0], size[1])

    def below(size, bound):
        return (size[0] <= bound) & (size[1] <= bound)

    start = (0, jnp.float32(1e3), jnp.float32(1e3))
    ended = lax.while_loop(
        lambda c: (c[0] < QUICK_STEPS) & jnp.logical_not(below(c[1:], 0.25)), quick, start
    )
    for k in range(2):

        @pl.when(jnp.logical_not(ended[k + 1] <= 0.25))
        def _():
            rows = jnp.sum(jnp.abs(scaled_ref[k]), axis=0, keepdims=True)
            x_ref[k] = unit / jnp.max(rows)

    def sure(carry):
        old = [x_ref[k] for k in range(2)]
        rest = [unit - full(scaled_ref[k], old[k]) for k in range(2)]
        size = [jnp.sum(r * r) for r in rest]
        more = [r + rough(r, r) for r in rest]
        for k in range(2):
            x_ref[k] = old[k] + full(old[k], more[k])
        return (carry[0] + 1, size[0], size[1])

    lax.while_loop(
        lambda c: (c[0] < SURE_STEPS) & jnp.logical_not(below(c[1:], 3e-4)), sure, start
    )
    return [x_ref[k] * down * along for k, (down, along) in enumerate(sides)]


def combine_into(a_ref, b_ref, out_ref, scaled_ref, x_ref):
    n = b_ref.shape[1]
    inverse = invert(a_ref[2 * n : 3 * n] + b_ref[0:n], scaled_ref, x_ref)
    x_ref[...] = inverse
    left = a_ref[n : 2 * n]
    right = b_ref[n : 2 * n]
    left_x = full(left, x_ref[...])
    x_right = full(x_ref[...], right)
    mid = a_ref[3 * n + 1 : 3 * n + 2] + b_ref[3 * n : 3 * n + 1]
    mid = jnp.broadcast_to(mid, (pad, n))
    out_ref[0:n] = a_ref[0:n] - full(left_x, left, 1, 1)
    out_ref[n : 2 * n] = -full(left_x, right)
    out_ref[2 * n : 3 * n] = b_ref[2 * n : 3 * n] - full(right, x_right, 0, 0)
    row = lax.broadcasted_iota(jnp.int32, (pad, n), 0)
    first = a_ref[3 * n : 3 * n + 1] - full(mid, left_x, 1, 1)
    second = b_ref[3 * n + 1 : 3 * n + 2] - full(mid, x_right)
    out_ref[3 * n : 3 * n + pad] = jnp.where(row == 0, first, jnp.where(row == 1, second, 0.0))


def combine_kernel(flag_ref, a_ref, b_ref, out_ref, scaled_ref, x_ref):
    @pl.when(flag_ref[0] == 0)
    def _():
        out_ref[...] = b_ref[...]

    @pl.when(flag_ref[0] != 0)
    def _():
        combine_into(a_ref, b_ref, out_ref, scaled_ref, x_ref)


def pack_half(core, src, half_ref):
    n = src.shape[1]

    @pl.when(core == 0)
    def _():
        half_ref[0:n] = src[n : 2 * n]
        half_ref[n : n + pad] = src[3 * n : 3 * n + pad]

    @pl.when(core != 0)
    def _():
        down = lax.broadcasted_iota(jnp.int32, (n, n), 0)
        along = lax.broadcasted_iota(jnp.int32, (n, n), 1)
        out = src[2 * n : 3 * n]
        half_ref[0:n] = jnp.where(down <= along, src[0:n], out)
        diagonal = jnp.sum(jnp.where(down == along, out, 0.0), axis=0, keepdims=True)
        row = lax.broadcasted_iota(jnp.int32, (pad, n), 0)
        half_ref[n : n + pad] = jnp.where(row == 2, diagonal, src[3 * n : 3 * n + pad])


def unpack(cross_ref, both_ref, dst):
    n = dst.shape[1]
    down = lax.broadcasted_iota(jnp.int32, (n, n), 0)
    along = lax.broadcasted_iota(jnp.int32, (n, n), 1)
    both = both_ref[0:n]
    flipped = both.T
    dst[0:n] = jnp.where(down <= along, both, flipped)
    dst[n : 2 * n] = cross_ref[0:n]
    out = jnp.where(down > along, both, flipped)
    dst[2 * n : 3 * n] = jnp.where(down == along, both_ref[n + 2 : n + 3], out)
    row = lax.broadcasted_iota(jnp.int32, (pad, n), 0)
    dst[3 * n : 3 * n + pad] = jnp.where(row < 2, both_ref[n : n + pad], 0.0)


def chip_kernel(core_ref, own_ref, other_ref, total_ref, half_ref, scaled_ref, x_ref):
    core = core_ref[0]

    @pl.when(core == 0)
    def _():
        combine_into(own_ref, other_ref, total_ref, scaled_ref, x_ref)

    @pl.when(core != 0)
    def _():
        combine_into(other_ref, own_ref, total_ref, scaled_ref, x_ref)

    pack_half(core, total_ref, half_ref)


def advance_into(a_ref, b_ref, out_ref, scaled_ref, x_ref):
    n = b_ref.shape[1]
    inverse = invert(a_ref[0:n] + b_ref[0:n], scaled_ref, x_ref)
    right = b_ref[n : 2 * n]
    x_right = full(inverse, right)
    mid = a_ref[n + 1 : n + 2] + b_ref[3 * n : 3 * n + 1]
    mid = jnp.broadcast_to(mid, (pad, n))
    out_ref[0:n] = b_ref[2 * n : 3 * n] - full(right, x_right, 0, 0)
    second = b_ref[3 * n + 1 : 3 * n + 2] - full(mid, x_right)
    row = lax.broadcasted_iota(jnp.int32, (pad, n), 0)
    out_ref[n : n + pad] = jnp.where(row == 1, second, 0.0)


def plane_kernel(
    place_ref, mine_ref, theirs_ref, own_ref, group_ref, chip_ref, state_ref, scaled_ref, x_ref
):
    n = own_ref.shape[1]

    @pl.when(place_ref[0] == 0)
    def _():
        unpack(mine_ref, theirs_ref, chip_ref)

    @pl.when(place_ref[0] != 0)
    def _():
        unpack(theirs_ref, mine_ref, chip_ref)

    @pl.when(place_ref[1] == 0)
    def _():
        combine_into(own_ref, chip_ref, group_ref, scaled_ref, x_ref)

    @pl.when(place_ref[1] != 0)
    def _():
        combine_into(chip_ref, own_ref, group_ref, scaled_ref, x_ref)

    state_ref[...] = group_ref[2 * n : 3 * n + pad]


def advance_kernel(flag_ref, a_ref, b_ref, out_ref, scaled_ref, x_ref):
    @pl.when(flag_ref[0] == 0)
    def _():
        n = b_ref.shape[1]
        out_ref[...] = b_ref[2 * n : 3 * n + pad]

    @pl.when(flag_ref[0] != 0)
    def _():
        advance_into(a_ref, b_ref, out_ref, scaled_ref, x_ref)


def last_kernel(flag_ref, a_ref, b_ref, c_ref, cov_ref, mean_ref, s_ref, scaled_ref, x_ref):
    n = a_ref.shape[1]
    both = (b_ref, c_ref)

    @pl.when(flag_ref[0] == 0)
    def _():
        for k, e_ref in enumerate(both):
            s_ref[k] = e_ref[2 * n : 3 * n + pad]

    @pl.when(flag_ref[0] != 0)
    def _():
        inverses = invert_pair([a_ref[0:n] + e_ref[0:n] for e_ref in both], scaled_ref, x_ref)
        row = lax.broadcasted_iota(jnp.int32, (pad, n), 0)
        for k, e_ref in enumerate(both):
            right = e_ref[n : 2 * n]
            x_right = full(inverses[k], right)
            mid = a_ref[n + 1 : n + 2] + e_ref[3 * n : 3 * n + 1]
            mid = jnp.broadcast_to(mid, (pad, n))
            s_ref[k, 0:n] = e_ref[2 * n : 3 * n] - full(right, x_right, 0, 0)
            second = e_ref[3 * n + 1 : 3 * n + 2] - full(mid, x_right)
            s_ref[k, n : n + pad] = jnp.where(row == 1, second, 0.0)

    covs = invert_pair([s_ref[k, 0:n] for k in range(2)], scaled_ref, x_ref)
    for k in range(2):
        cov_ref[k] = covs[k]
        mean_ref[k] = full(s_ref[k, n : n + pad], covs[k], 1, 1)


vmem = pl.BlockSpec(memory_space=pltpu.VMEM)
smem = pl.BlockSpec(memory_space=pltpu.SMEM)


def call(kernel, specs, shapes, n, *extra, wide=()):
    return pl.pallas_call(
        kernel,
        out_shape=shapes,
        in_specs=specs,
        out_specs=jax.tree.map(lambda unused: vmem, shapes),
        scratch_shapes=[*extra] + [pltpu.VMEM((*wide, n, n), jnp.float32)] * 2,
        compiler_params=pltpu.CompilerParams(vmem_limit_bytes=40 * 1024 * 1024),
        cost_estimate=pl.CostEstimate(flops=20_000_000_000, bytes_accessed=3_000_000, transcendentals=0),
    )


def f32(*shape):
    return jax.ShapeDtypeStruct(shape, jnp.float32)


def combine(flag, earlier, later):
    n = later.shape[1]
    return call(combine_kernel, [smem, vmem, vmem], f32(3 * n + pad, n), n)(flag, earlier, later)


def advance(flag, earlier, later):
    n = later.shape[1]
    return call(advance_kernel, [smem, vmem, vmem], f32(n + pad, n), n)(flag, earlier, later)


def chip_total(core, own, other):
    n = own.shape[1]
    shapes = (f32(3 * n + pad, n), f32(n + pad, n))
    return call(chip_kernel, [smem, vmem, vmem], shapes, n)(core, own, other)


def plane_total(place, mine, theirs, own):
    n = own.shape[1]
    shapes = (f32(3 * n + pad, n), f32(3 * n + pad, n), f32(n + pad, n))
    return call(plane_kernel, [smem, vmem, vmem, vmem], shapes, n)(place, mine, theirs, own)


def filtered(flag, earlier, first, second):
    n = earlier.shape[1]
    return call(
        last_kernel,
        [smem, vmem, vmem, vmem],
        (f32(2, n, n), f32(2, pad, n)),
        n,
        pltpu.VMEM((2, n + pad, n), jnp.float32),
        wide=(2,),
    )(flag, earlier, first, second)


def gram_kernel(x_ref, out_ref):
    peers, n = x_ref.shape[1], x_ref.shape[4]
    sensors = x_ref.shape[3] - extra
    half = n // 2
    rows = x_ref[0, :, 0, 0:sensors, :].reshape(peers * sensors, n)
    gram = lax.dot_general(
        rows, rows, (((0,), (0,)), ((), ())), preferred_element_type=jnp.float32
    )
    out_ref[0, 0, 0:half] = gram[0:half]
    out_ref[0, 0, half : half + half // 2, 0:half] = gram[half : half + half // 2, half:]
    out_ref[0, 0, half : half + half // 2, half:] = gram[half + half // 2 :, half:]
    tail = x_ref[0, :, 0, sensors:, :].astype(jnp.float32).reshape(peers * extra, n)
    info = jnp.sum(tail, axis=0, keepdims=True)
    out_ref[0, 0, half + half // 2 :] = jnp.broadcast_to(info, (pad, n))


def gram_terms(rows):
    blocks, peers, steps, height, n = rows.shape
    tall = n // 2 + n // 4 + pad
    return pl.pallas_call(
        gram_kernel,
        grid=(blocks, steps),
        out_shape=f32(blocks, steps, tall, n),
        in_specs=[pl.BlockSpec((1, peers, 1, height, n), lambda i, j: (i, 0, j, 0, 0))],
        out_specs=pl.BlockSpec((1, 1, tall, n), lambda i, j: (i, j, 0, 0)),
        compiler_params=pltpu.CompilerParams(vmem_limit_bytes=24 * 1024 * 1024),
    )(rows)


def whole_gram(packed):
    n = packed.shape[1]
    half, quarter = n // 2, n // 4
    low = packed[half : half + quarter]
    corner = jnp.concatenate([low[:, :half], low[:, half:]], axis=0)
    top = packed[:half]
    return jnp.concatenate([top, jnp.concatenate([top[:, half:].T, corner], axis=1)], axis=0)


def three_terms(x):
    high = lax.reduce_precision(x, 8, 7)
    rest = x - high
    middle = lax.reduce_precision(rest, 8, 7)
    return jnp.stack([high, middle, rest - middle], axis=1).astype(jnp.bfloat16)


def swap(x, axis):
    return lax.ppermute(x, axis, [(0, 1), (1, 0)])


def flag(*values):
    return jnp.stack([jnp.asarray(value, jnp.int32) for value in values])


def body(obs_rows, readings, available, sensor_ids, noise_var, col_scale, transition, process_info):
    n = obs_rows.shape[2]
    sensor_total = noise_var.shape[0]
    lookup_table = (
        sensor_ids[:, None] == jnp.arange(sensor_total, dtype=jnp.int32)[None, :]
    ).astype(jnp.float32)
    local_var = matmul(lookup_table, noise_var)
    weight = available.astype(jnp.float32) * lax.rsqrt(local_var)[None, :]
    weighted = (obs_rows.astype(jnp.float32) * weight[:, :, None]).astype(jnp.bfloat16)
    signal = (readings * weight).astype(jnp.bfloat16)
    own_info = jnp.einsum("tm,tms->ts", signal, weighted, preferred_element_type=jnp.float32)
    steps = obs_rows.shape[0]
    planes, plane_size = lax.axis_size("tm"), lax.axis_size(("sensor", "state"))
    block_len = steps // (planes * plane_size)
    terms = three_terms(own_info)
    terms = jnp.pad(terms, ((0, 0), (0, extra - terms.shape[1]), (0, 0)))
    sent = jnp.concatenate([weighted, terms], axis=1)
    sent = sent.reshape(planes, plane_size, block_len, sent.shape[1], n)
    packed = []
    for k in range(block_len):
        arrived = lax.all_to_all(
            sent[:, :, k : k + 1], ("sensor", "state"), split_axis=1, concat_axis=1, tiled=True
        )
        packed.append(
            lax.psum_scatter(gram_terms(arrived), "tm", scatter_dimension=0, tiled=True)[0, 0]
        )
    gram_part = [whole_gram(packed[k]) for k in range(block_len)]
    info_part = [part[n // 2 + n // 4] for part in packed]
    mine = lax.axis_index(everyone)
    carried = matmul(process_info, transition)
    inward = matmul(transition.T, carried)
    outer_scale = col_scale[:, None] * col_scale[None, :]

    def element(k):
        keep = (mine * block_len + k > 0).astype(jnp.float32)
        vectors = jnp.concatenate(
            [
                jnp.zeros((1, n), jnp.float32),
                (info_part[k] * col_scale)[None, :],
                jnp.zeros((pad - 2, n), jnp.float32),
            ]
        )
        return jnp.concatenate(
            [
                inward * keep,
                carried.T * -keep,
                process_info + gram_part[k] * outer_scale,
                vectors,
            ]
        )

    elements = [element(k) for k in range(block_len)]
    summary = combine(flag(1), elements[0], elements[1])

    core = lax.axis_index("state")
    chips, chip = lax.axis_size("sensor"), lax.axis_index("sensor")
    planes, plane = lax.axis_size("tm"), lax.axis_index("tm")
    other = swap(summary, "state")
    own_chip, half = chip_total(flag(core), summary, other)
    if chips == 2:
        mine_half = swap(half, "sensor")
        theirs_half = swap(mine_half, "state")
        group, prior, state = plane_total(flag(core, chip), mine_half, theirs_half, own_chip)
        has_prior = chip > 0
    else:
        everything = lax.all_gather(own_chip, "sensor")
        group, prior = everything[0], everything[0]
        for k in range(1, chips):
            group = combine(flag(1), group, everything[k])
            if k < chips - 1:
                prior = jnp.where(k < chip, group, prior)
        has_prior = chip > 0
        state = group[2 * n :]

    incoming = jnp.zeros_like(state)
    for k in range(1, planes):
        perm = [(k - 1, k)]
        came = lax.ppermute(state, "tm", perm)
        if k < planes - 1:
            state = advance(flag(plane == k), came, group)
        incoming = incoming + came

    ahead = combine(flag(has_prior & (core > 0)), prior, other)
    ahead = jnp.where(core > 0, ahead, prior)
    has_ahead = has_prior | (core > 0)
    first = combine(flag(has_ahead), ahead, elements[0])
    second = combine(flag(has_ahead), ahead, summary)
    covs, means = filtered(flag(plane > 0), incoming, first, second)
    return (means[:, 1], covs)


def solution(mesh):
    in_specs = (
        P("groups", ("tm", "sensor", "state"), None),
        P("groups", ("tm", "sensor", "state")),
        P("groups", ("tm", "sensor", "state")),
        P(("groups", "tm", "sensor", "state")),
        P(),
        P(),
        P(),
        P(),
    )
    out_specs = (
        P(("groups", "tm", "sensor", "state"), None),
        P(("groups", "tm", "sensor", "state"), None, None),
    )
    return jax.shard_map(body, mesh=mesh, in_specs=in_specs, out_specs=out_specs, check_vma=False)
```
